256 devices in a mesh: dp: 32 (over y_hi, z, core), vocab: 8 (over y_lo, x).
Axes of the slice: x: 4, y: 4 (y_hi: 2, y_lo: 2; y = y_hi * 2 + y_lo), z: 8, core: 2. Of those that a mesh axis runs over, the one named last changes fastest.
Arguments:
- hidden: bfloat16 [512, 8192], P('dp'), may hold values from -6 to 6
- head: bfloat16 [65536, 8192], P('vocab', 'dp'), may hold values from -0.0625 to 0.0625
- targets: int32 [512], P('dp'), may hold values from -1 to 65535, as said below
- log_norm: float32 [512], P('dp'), may hold values from 1 to 9
- loss_scale: float32 [], replicated, may hold values from 64 to 512
Outputs:
- grad_hidden: bfloat16 [512, 8192], P('dp')
- grad_head: bfloat16 [65536, 8192], P('vocab', 'dp')
- loss: float32 [], replicated
The draws below stay inside these ranges and needn't reach their ends.
Inputs may be any that keep to these rules, and one draw needn't show every extreme that they name: `targets`: the first token of each group of 16 tokens is always kept.
All inputs are finite; a program needn't handle non-finite values.
Results may differ from the reference program's by a relative error of at most 0.0045.
Values may be sent and summed in bfloat16 or wider, within the bound.
No kernel may reach another device: no remote copies, remote signals or barrier semaphores. Data moves between devices by JAX's collectives and lax.ppermute only.
A program may use at most 128 MiB of HBM per device.

```python
import math
import jax
import jax.numpy as jnp

D = 8192
TOK_DEV = 16
V = 65536
TOKENS = 512


def draw_targets(key, part):
    key = jax.random.fold_in(key, 11)
    key_ids, key_kept = jax.random.split(key)
    token_ids = jax.random.randint(key_ids, (TOKENS,), 0, V, dtype=jnp.int32)
    rolled = jax.random.randint(key_kept, (TOKENS,), 0, 1000, dtype=jnp.int32)
    position = jnp.arange(TOKENS, dtype=jnp.int32)
    group_index = position // TOK_DEV
    groups = max(TOKENS // TOK_DEV - 1, 1)
    threshold = 250 + 500 * group_index // groups
    kept_token = (rolled < threshold) | (position % TOK_DEV == 0)
    return jnp.where(kept_token, token_ids, -1).astype(jnp.int32)


def draw_log_norm(key, part):
    key = jax.random.fold_in(key, 12)
    centre = 0.5 * math.log(V) + 1.0
    unit = jax.random.uniform(key, (TOKENS,), jnp.float32, -1.0, 1.0)
    return (centre + 0.5 * unit).astype(jnp.float32)


def level_of(own_key, shape, cuts, smallest, largest):
    loudness, own = 1.0, jax.random.fold_in(own_key, 6)
    for axis_at, parts in cuts:
        draws = jnp.exp(jax.random.uniform(jax.random.fold_in(own, axis_at), (parts,), jnp.float32, smallest / len(cuts), largest / len(cuts)))
        loudness = loudness * jnp.repeat(draws, shape[axis_at] // parts).reshape([-1 if axis == axis_at else 1 for axis in range(len(shape))])
    return loudness


def normal_values(own_key, shape, width, bound, pieces=(), held_as=jnp.bfloat16):
    level = level_of(own_key, shape, pieces, -0.22, 0.18) if pieces else 1.0
    result = jax.random.normal(own_key, shape, jnp.float32) * width * level
    return jnp.minimum(jnp.maximum(result, -bound), bound).astype(held_as)


def setup_inputs(seed: int = 0) -> dict:
    streams_of = jax.random.split(jax.random.key(seed), 6)
    hidden = normal_values(streams_of[0], (TOKENS, D), 1.0, 6.0, ((0, 32),))
    head = normal_values(streams_of[1], (V, D), D ** -0.5, 0.0625, ((0, 8), (1, 32)))
    targets = draw_targets(jax.random.fold_in(streams_of[5], 71), 0)
    log_norm = draw_log_norm(jax.random.fold_in(streams_of[5], 71), 0)
    loss_scale = jnp.clip(jnp.exp(jax.random.uniform(streams_of[4], (), jnp.float32, math.log(64.0), math.log(512.0))), 64.0, 512.0)
    return {"hidden": hidden, "head": head, "targets": targets, "log_norm": log_norm, "loss_scale": loss_scale}


def reference(hidden, head, targets, log_norm, loss_scale):
    logits = jnp.dot(hidden, head.T, preferred_element_type=jnp.float32)
    vocab_ids = jnp.arange(V, dtype=jnp.int32)
    onehot = vocab_ids[None, :] == targets[:, None]
    kept = targets >= 0
    probs = jnp.exp(logits - log_norm[:, None])
    grad_logits = jnp.where(kept[:, None], probs - onehot.astype(jnp.float32), jnp.float32(0.0)).astype(jnp.bfloat16)
    count = jnp.sum(kept.astype(jnp.float32))
    factor = loss_scale / count
    grad_head = (jnp.dot(grad_logits.T, hidden, preferred_element_type=jnp.float32) * factor).astype(jnp.bfloat16)
    grad_hidden = (jnp.dot(grad_logits, head, preferred_element_type=jnp.float32) * factor).astype(jnp.bfloat16)
    target_sum = jnp.sum(jnp.where(onehot, logits, jnp.float32(0.0)))
    norm_sum = jnp.sum(jnp.where(kept, log_norm, jnp.float32(0.0)))
    loss = (norm_sum - target_sum) / count
    return grad_hidden, grad_head, loss
```

```python
import jax
import jax.numpy as jnp
from jax import lax
from jax.sharding import Mesh, PartitionSpec as P

F32 = jnp.float32
BF16 = jnp.bfloat16
F16 = jnp.float16
DP = ("yh", "z", "c")
VOCAB = ("yl", "x")
RING = 8
STREAMS = 2


def swap(value, axis):
    return lax.ppermute(value, axis, [(0, 1), (1, 0)])


def hop(value, step):
    return lax.ppermute(value, "z", [(i, (i + step) % RING) for i in range(RING)])


def dot(a, b, contract):
    return lax.dot_general(a, b, (contract, ((), ())), preferred_element_type=F32)


def three(value):
    high = value.astype(BF16)
    rest = value - high.astype(F32)
    mid = rest.astype(BF16)
    low = (rest - mid.astype(F32)).astype(BF16)
    return [high, mid, low]


def on_device(hidden, head, targets, log_norm, loss_scale):
    rows, width = head.shape
    half = rows // 2
    tokens_own = hidden.shape[0]
    groups = lax.axis_size(DP)
    vocab_size = lax.axis_size(VOCAB)
    core = lax.axis_index("c")
    yh = lax.axis_index("yh")
    z = lax.axis_index("z")
    vocab_index = lax.axis_index(VOCAB)
    tokens = groups * tokens_own
    chunk = half // RING
    quarter = chunk // 2
    span = tokens // STREAMS

    facts = jnp.stack([targets.astype(F32), log_norm], axis=0)[None]
    facts = lax.all_gather(facts, DP, axis=0, tiled=True)
    all_targets = facts[:, 0].reshape(-1).astype(jnp.int32)
    all_norms = facts[:, 1].reshape(-1)
    kept = all_targets >= 0
    count = jnp.sum(kept.astype(F32))
    factor = loss_scale / count

    head_sib = swap(lax.dynamic_slice_in_dim(head, (1 - core) * half, half, 0), "c")
    hid_own = lax.all_to_all(hidden, DP, split_axis=1, concat_axis=0, tiled=True)
    hid_sib = swap(hid_own, "c")

    def partial(distance, s):
        place = lax.rem(z + distance + RING, RING) * chunk
        own = lax.dynamic_slice_in_dim(head, core * half + place, chunk, 0)
        sib = lax.dynamic_slice_in_dim(head_sib, place, chunk, 0)
        t = slice(s * span, (s + 1) * span)
        return dot(own, hid_own[t], ((1,), (1,))) + dot(sib, hid_sib[t], ((1,), (1,)))

    sums = []
    for s in range(STREAMS):
        way = 1 if s % 2 == 0 else -1
        ends = []
        for direction, length in ((way, RING // 2), (-way, RING // 2 - 1)):
            got = None
            for distance in range(length, 0, -1):
                term = partial(direction * distance, s)
                if got is not None:
                    term = term + got.astype(F32)
                got = hop(term.astype(F16), direction)
            ends.append(got)
        sums.append(partial(0, s) + ends[0].astype(F32) + ends[1].astype(F32))

    first = vocab_index * rows + core * half + z * chunk + yh * quarter
    ids = first + jnp.arange(quarter, dtype=jnp.int32)
    mine, target_sum = [], 0.0
    for s in range(STREAMS):
        t = slice(s * span, (s + 1) * span)
        keep = lax.dynamic_slice_in_dim(sums[s], yh * quarter, quarter, 0)
        give = lax.dynamic_slice_in_dim(sums[s], (1 - yh) * quarter, quarter, 0)
        logits = keep + swap(give.astype(F16), "yh").astype(F32)
        onehot = ids[:, None] == all_targets[None, t]
        probs = jnp.exp(logits - all_norms[None, t])
        mine.append(jnp.where(kept[None, t], probs - onehot.astype(F32), 0.0).astype(BF16))
        target_sum += jnp.sum(jnp.where(onehot, logits, 0.0))

    pieces = {}
    for s in range(STREAMS):
        way = 1 if s % 2 == 0 else -1
        for q, piece in ((0, mine[s]), (1, swap(mine[s], "yh"))):
            pieces[s, q, 0] = piece
            for direction, length in ((way, RING // 2), (-way, RING // 2 - 1)):
                got = piece
                for distance in range(1, length + 1):
                    got = hop(got, direction)
                    pieces[s, q, (-direction * distance) % RING] = got

    gh = {}
    hidden_grad = 0.0
    grad_head = jnp.zeros((rows, width), BF16)
    for distance in range(RING):
        for q in range(2):
            piece = jnp.concatenate([pieces[s, q, distance] for s in range(STREAMS)], axis=1)
            other = swap(piece, "c")
            at = lax.rem(z + distance, RING) * chunk + (yh if q == 0 else 1 - yh) * quarter
            for block, base in ((piece, core * half), (other, (1 - core) * half)):
                place = base + at
                result = (dot(block, hid_own, ((1,), (0,))) * factor).astype(BF16)
                grad_head = lax.dynamic_update_slice_in_dim(grad_head, result, place, 0)
                rows_here = lax.dynamic_slice_in_dim(head, place, quarter, 0)
                hidden_grad += dot(block, rows_here, ((0,), (0,)))

    share = tokens_own // vocab_size
    terms = hidden_grad.reshape(groups, vocab_size, share, width).transpose(1, 0, 2, 3)
    terms = terms.reshape(vocab_size, groups * share, width)
    extra = jnp.broadcast_to(target_sum, (vocab_size, 8, width))
    terms = jnp.concatenate([terms, extra], axis=1)
    terms = lax.all_to_all(terms, VOCAB, split_axis=0, concat_axis=0, tiled=True)
    terms = jnp.sum(terms, axis=0)
    total = (terms[: groups * share] * factor).astype(BF16).reshape(groups, share, width)
    parts = jnp.stack(three(terms[groups * share]) + [jnp.zeros((width,), BF16)], axis=0)
    parts = jnp.broadcast_to(parts, (groups,) + parts.shape)
    mine = lax.all_to_all(
        jnp.concatenate([total, parts], axis=1), DP, split_axis=0, concat_axis=0, tiled=True)
    sums = jnp.sum(mine[:, share:, 0].astype(F32))
    mine = mine[:, :share].transpose(1, 0, 2).reshape(1, share, groups * width)
    grad_hidden = lax.all_to_all(
        jnp.broadcast_to(mine, (vocab_size,) + mine.shape[1:]), VOCAB,
        split_axis=0, concat_axis=0, tiled=True).reshape(tokens_own, groups * width)

    norm_sum = jnp.sum(jnp.where(kept, all_norms, 0.0))
    loss = (norm_sum - sums) / count
    return grad_hidden, grad_head, loss


def solution(mesh):
    fine = Mesh(mesh.devices.reshape(2, RING, 2, 2, 4), ("yh", "z", "c", "yl", "x"))
    return jax.shard_map(
        on_device,
        mesh=fine,
        in_specs=(P(DP, None), P(VOCAB, DP), P(DP), P(DP), P()),
        out_specs=(P(DP, None), P(VOCAB, DP), P()),
        check_vma=False,
    )
```

```python
import jax
import jax.numpy as jnp
from jax import lax
from jax.sharding import Mesh, PartitionSpec as P

F32 = jnp.float32
BF16 = jnp.bfloat16
F16 = jnp.float16
DP = ("yh", "z", "c")
CHIPS = ("yh", "z")
VOCAB = ("yl", "x")
RING = 8
FACT_ROWS = 8


def swap(value, axis):
    return lax.ppermute(value, axis, [(0, 1), (1, 0)])


def hop(value, step):
    return lax.ppermute(value, "z", [(i, (i + step) % RING) for i in range(RING)])


def dot(a, b, contract):
    return lax.dot_general(a, b, (contract, ((), ())), preferred_element_type=F32)


def exchange(value, axes):
    return lax.all_to_all(value, axes, split_axis=0, concat_axis=0, tiled=True)


def three(value):
    high = lax.reduce_precision(value, 8, 7)
    mid = lax.reduce_precision(value - high, 8, 7)
    return [part.astype(BF16) for part in (high, mid, value - high - mid)]


def flip(value, which, axis):
    first, second = jnp.split(value, 2, axis)
    return jnp.where(which == 0, value, jnp.concatenate([second, first], axis))


def on_device(hidden, head, targets, log_norm, loss_scale):
    rows, width = head.shape
    half = rows // 2
    tokens_own, features = hidden.shape
    chips = lax.axis_size(CHIPS)
    vocab_size = lax.axis_size(VOCAB)
    core = lax.axis_index("c")
    yh = lax.axis_index("yh")
    z = lax.axis_index("z")
    vocab_index = lax.axis_index(VOCAB)
    chunk = half // RING
    quarter = chunk // 2
    pair = 2 * width
    span = chips * tokens_own

    code = targets + 1
    facts = jnp.stack([(code // 256).astype(BF16), (code % 256).astype(BF16)] + three(log_norm))
    facts = jnp.pad(facts, ((0, FACT_ROWS - facts.shape[0]), (0, pair - tokens_own)))
    sent = hidden.reshape(tokens_own, chips, pair).transpose(1, 0, 2)
    sent = jnp.concatenate([sent, jnp.broadcast_to(facts, (chips,) + facts.shape)], axis=1)
    got = exchange(sent, CHIPS)
    both = [got, swap(got, "c")]

    def rolled(which):
        parts = []
        for distance in range(RING):
            place = which * half + lax.rem(z + distance, RING) * chunk
            for q in (yh, 1 - yh):
                parts.append(lax.dynamic_slice_in_dim(head, place + q * quarter, quarter, 0))
        return jnp.concatenate(parts, 0)

    wide = jnp.concatenate([rolled(core), swap(rolled(1 - core), "c")], axis=1)

    hid, target, norm = [], [], []
    for value in both:
        hid.append(flip(value[:, :tokens_own].reshape(span, pair), core, 1))
        f = value[:, tokens_own:, :tokens_own].astype(F32).transpose(1, 0, 2).reshape(FACT_ROWS, span)
        target.append((f[0] * 256.0 + f[1]).astype(jnp.int32) - 1)
        norm.append(f[2] + f[3] + f[4])
    count = sum(jnp.sum((t >= 0).astype(F32)) for t in target)
    norm_sum = sum(jnp.sum(jnp.where(t >= 0, n, 0.0)) for t, n in zip(target, norm))
    factor = loss_scale / count

    def head_chunk(distance):
        at = distance % RING * chunk
        return wide[at : at + chunk]

    grad, target_sum = [], 0.0
    first = vocab_index * rows + core * half + z * chunk + yh * quarter
    ids = first + jnp.arange(quarter, dtype=jnp.int32)
    for s in range(2):
        way = 1 if s == 0 else -1
        total = None
        for direction, length in ((way, RING // 2), (-way, RING // 2 - 1)):
            arrived = None
            for distance in range(length, 0, -1):
                term = dot(hid[s], head_chunk(direction * distance), ((1,), (1,)))
                if arrived is not None:
                    term = term + arrived.astype(F32)
                arrived = hop(term.astype(F16), direction)
            total = arrived.astype(F32) if total is None else total + arrived.astype(F32)
        total = total + dot(hid[s], head_chunk(0), ((1,), (1,)))
        logits = total[:, :quarter] + swap(total[:, quarter:].astype(F16), "yh").astype(F32)
        onehot = ids[None, :] == target[s][:, None]
        probs = jnp.exp(logits - norm[s][:, None])
        grad.append(
            jnp.where(target[s][:, None] >= 0, probs - onehot.astype(F32), 0.0).astype(BF16))
        target_sum += jnp.sum(jnp.where(onehot, logits, 0.0))
    target_sum = target_sum + swap(target_sum, "c")

    pieces = {}
    for s in range(2):
        way = 1 if s == 0 else -1
        for q, piece in ((0, grad[s]), (1, swap(grad[s], "yh"))):
            pieces[s, q, 0] = piece
            for direction, length in ((way, RING // 2), (-way, RING // 2 - 1)):
                arrived = piece
                for distance in range(1, length + 1):
                    arrived = hop(arrived, direction)
                    pieces[s, q, (-direction * distance) % RING] = arrived

    def gathered(s, distances):
        return jnp.concatenate([pieces[s, q, d] for d in distances for q in range(2)], axis=1)

    batches = ((0, 1, 7), (2, 6), (3, 4, 5))
    blocks = {(s, b): gathered(s, b) for b in batches for s in range(2)}
    hidden_grad = [0.0, 0.0]
    for b in batches:
        rows_here = jnp.concatenate([head_chunk(d) for d in b], axis=0)
        for s in (1, 0):
            hidden_grad[s] += dot(blocks[s, b], rows_here, ((1,), (0,)))

    made = {}
    for b in batches:
        value = dot(blocks[0, b], hid[0], ((0,), (0,))) + dot(blocks[1, b], hid[1], ((0,), (0,)))
        value = (value * factor).astype(BF16)
        for i, d in enumerate(b):
            made[d] = value[i * chunk : (i + 1) * chunk]
    made = jnp.concatenate([made[d] for d in range(RING)], axis=0)
    gh_own, gh_sib = made[:, :width], swap(made[:, width:], "c")
    grad_head = jnp.zeros((rows, width), BF16)
    for value, which in ((gh_own, core), (gh_sib, 1 - core)):
        for distance in range(RING):
            place = which * half + lax.rem(z + distance, RING) * chunk
            part = flip(value[distance * chunk : (distance + 1) * chunk], yh, 0)
            grad_head = lax.dynamic_update_slice_in_dim(grad_head, part, place, 0)

    other = swap(hidden_grad[1], "c")
    mine = hidden_grad[0] + jnp.concatenate([other[:, width:], other[:, :width]], axis=1)
    share = tokens_own // vocab_size
    terms = mine.reshape(chips, vocab_size, share, pair).transpose(1, 0, 2, 3)
    terms = terms.reshape(vocab_size, chips * share, pair)
    terms = jnp.concatenate([terms, jnp.broadcast_to(target_sum, (vocab_size, 8, pair))], axis=1)
    terms = jnp.sum(exchange(terms, VOCAB), axis=0)
    total = (terms[: chips * share] * factor).astype(BF16).reshape(chips, share, pair)
    total = flip(total, core, 2)
    parts = jnp.stack(three(terms[chips * share]) + [jnp.zeros((pair,), BF16)], axis=0)
    parts = jnp.broadcast_to(parts, (chips,) + parts.shape)
    mine = exchange(jnp.concatenate([total, parts], axis=1), CHIPS)
    sums = jnp.sum(mine[:, share:, 0].astype(F32))
    mine = mine[:, :share].transpose(1, 0, 2).reshape(1, share, features)
    grad_hidden = exchange(
        jnp.broadcast_to(mine, (vocab_size, share, features)), VOCAB).reshape(tokens_own, features)

    loss = (norm_sum - sums) / count
    return grad_hidden, grad_head, loss


def solution(mesh):
    fine = Mesh(mesh.devices.reshape(2, RING, 2, 2, 4), ("yh", "z", "c", "yl", "x"))
    return jax.shard_map(
        on_device,
        mesh=fine,
        in_specs=(P(DP, None), P(VOCAB, DP), P(DP), P(DP), P()),
        out_specs=(P(DP, None), P(VOCAB, DP), P()),
        check_vma=False,
    )
```

```python
import jax
import jax.numpy as jnp
from jax import lax
from jax.experimental import pallas as pl
from jax.experimental.pallas import tpu as pltpu
from jax.sharding import Mesh, PartitionSpec as P

F32 = jnp.float32
BF16 = jnp.bfloat16
F16 = jnp.float16
DP = ("yh", "z", "c")
CHIPS = ("yh", "z")
VOCAB = ("yl", "x")
RING = 8
FACT_ROWS = 8


def swap(value, axis):
    return lax.ppermute(value, axis, [(0, 1), (1, 0)])


def hop(value, step):
    return lax.ppermute(value, "z", [(i, (i + step) % RING) for i in range(RING)])


def dot(a, b, contract):
    return lax.dot_general(a, b, (contract, ((), ())), preferred_element_type=F32)


def exchange(value, axes):
    return lax.all_to_all(value, axes, split_axis=0, concat_axis=0, tiled=True)


def three(value):
    high = lax.reduce_precision(value, 8, 7)
    mid = lax.reduce_precision(value - high, 8, 7)
    return [part.astype(BF16) for part in (high, mid, value - high - mid)]


def flip(value, which, axis):
    first, second = jnp.split(value, 2, axis)
    return jnp.where(which == 0, value, jnp.concatenate([second, first], axis))


def head_rows(pieces, hid, factor, core, z, rows, width):
    half = rows // 2
    chunk = half // RING

    def kernel(places, scale, *refs):
        pieces, (hid_a, hid_b, own, give, held, sems) = refs[: 2 * RING], refs[2 * RING :]
        copies = [None, None]
        for d in range(RING):
            slot = d % 2
            if copies[slot] is not None:
                for copy in copies[slot]:
                    copy.wait()
            made = dot(pieces[d][...], hid_a[...], ((0,), (0,)))
            made += dot(pieces[RING + d][...], hid_b[...], ((0,), (0,)))
            held[slot] = (made * scale[0]).astype(BF16)
            at = pl.multiple_of(places[d], chunk)
            copies[slot] = (
                pltpu.make_async_copy(
                    held.at[slot, :, pl.ds(0, width)],
                    own.at[pl.ds(pl.multiple_of(places[RING] + at, chunk), chunk)], sems.at[slot, 0]),
                pltpu.make_async_copy(
                    held.at[slot, :, pl.ds(width, width)],
                    give.at[pl.ds(at, chunk)], sems.at[slot, 1]),
            )
            for copy in copies[slot]:
                copy.start()
        for pair in copies:
            for copy in pair:
                copy.wait()

    order = lax.rem(z + jnp.arange(RING, dtype=jnp.int32), RING) * chunk
    places = jnp.concatenate([order, (core * half).reshape(1).astype(jnp.int32)])
    smem = pl.BlockSpec(memory_space=pltpu.SMEM)
    vmem = pl.BlockSpec(memory_space=pltpu.VMEM)
    return pl.pallas_call(
        kernel,
        out_shape=(
            jax.ShapeDtypeStruct((rows, width), BF16), jax.ShapeDtypeStruct((half, width), BF16)),
        in_specs=[smem, smem] + [vmem] * (2 * RING + 2),
        out_specs=(pl.BlockSpec(memory_space=pl.ANY), pl.BlockSpec(memory_space=pl.ANY)),
        scratch_shapes=[
            pltpu.VMEM((2, chunk, 2 * width), BF16),
            pltpu.SemaphoreType.DMA((2, 2)),
        ],
        compiler_params=pltpu.CompilerParams(vmem_limit_bytes=32 * 1024 * 1024),
        cost_estimate=pl.CostEstimate(
            flops=4 * hid[0].shape[0] * half * 2 * width, bytes_accessed=9 << 20, transcendentals=0),
        name="head_rows",
    )(places, factor.reshape(1), *pieces, *hid)


def on_device(hidden, head, targets, log_norm, loss_scale):
    rows, width = head.shape
    half = rows // 2
    tokens_own, features = hidden.shape
    chips = lax.axis_size(CHIPS)
    vocab_size = lax.axis_size(VOCAB)
    core = lax.axis_index("c")
    yh = lax.axis_index("yh")
    z = lax.axis_index("z")
    vocab_index = lax.axis_index(VOCAB)
    chunk = half // RING
    pair = 2 * width
    span = chips * tokens_own

    code = targets + 1
    facts = jnp.stack([(code // 256).astype(BF16), (code % 256).astype(BF16)] + three(log_norm))
    facts = jnp.pad(facts, ((0, FACT_ROWS - facts.shape[0]), (0, pair - tokens_own)))
    sent = hidden.reshape(tokens_own, chips, pair).transpose(1, 0, 2)
    sent = jnp.concatenate([sent, jnp.broadcast_to(facts, (chips,) + facts.shape)], axis=1)
    got = exchange(sent, CHIPS)
    both = [got, swap(got, "c")]

    own = lax.dynamic_slice_in_dim(head, core * half, half, 0)
    away = lax.dynamic_slice_in_dim(head, (1 - core) * half, half, 0)
    wide = jnp.concatenate([own, swap(away, "c")], axis=1)

    hid, target, norm = [], [], []
    for value in both:
        hid.append(flip(value[:, :tokens_own].reshape(span, pair), core, 1))
        f = value[:, tokens_own:, :tokens_own].astype(F32).transpose(1, 0, 2).reshape(FACT_ROWS, span)
        target.append((f[0] * 256.0 + f[1]).astype(jnp.int32) - 1)
        norm.append(f[2] + f[3] + f[4])
    count = sum(jnp.sum((t >= 0).astype(F32)) for t in target)
    norm_sum = sum(jnp.sum(jnp.where(t >= 0, n, 0.0)) for t, n in zip(target, norm))
    factor = loss_scale / count

    def place(distance):
        return lax.rem(z + distance + RING, RING) * chunk

    def head_chunk(distance):
        return lax.dynamic_slice_in_dim(wide, place(distance), chunk, 0)

    grad, target_sum = [], 0.0
    first = vocab_index * rows + core * half + z * chunk
    ids = first + jnp.arange(chunk, dtype=jnp.int32)
    for s in range(2):
        way = 1 if s == 0 else -1
        total = None
        for direction, length in ((way, RING // 2), (-way, RING // 2 - 1)):
            arrived = None
            for distance in range(length, 0, -1):
                term = dot(hid[s], head_chunk(direction * distance), ((1,), (1,)))
                if arrived is not None:
                    term = term + arrived.astype(F32)
                arrived = hop(term.astype(F16), direction)
            total = arrived.astype(F32) if total is None else total + arrived.astype(F32)
        total = total + dot(hid[s], head_chunk(0), ((1,), (1,)))
        logits = total + swap(total.astype(F16), "yh").astype(F32)
        onehot = ids[None, :] == target[s][:, None]
        probs = jnp.exp(logits - norm[s][:, None])
        grad.append(
            jnp.where(target[s][:, None] >= 0, probs - onehot.astype(F32), 0.0).astype(BF16))
        target_sum += jnp.sum(jnp.where(onehot, logits, 0.0))
    target_sum = jnp.where(yh == 0, target_sum, 0.0)
    target_sum = target_sum + swap(target_sum, "c")

    pieces = {}
    hidden_grad = [None, None]
    for s in range(2):
        way = 1 if s == 0 else -1
        pieces[s, 0] = grad[s]
        for direction, length in ((way, RING // 2), (-way, RING // 2 - 1)):
            arrived = grad[s]
            for distance in range(1, length + 1):
                arrived = hop(arrived, direction)
                pieces[s, (-direction * distance) % RING] = arrived
        for distance in (0, 1, 7, 2, 6, 3, 5, 4):
            term = dot(pieces[s, distance], head_chunk(distance), ((1,), (0,)))
            hidden_grad[s] = term if hidden_grad[s] is None else hidden_grad[s] + term

    grad_head, give = head_rows(
        [pieces[s, d] for s in range(2) for d in range(RING)], hid, factor, core, z, rows, width)
    grad_head = lax.dynamic_update_slice_in_dim(grad_head, swap(give, "c"), (1 - core) * half, 0)

    other = swap(hidden_grad[1], "c")
    mine = hidden_grad[0] + jnp.concatenate([other[:, width:], other[:, :width]], axis=1)
    share = tokens_own // vocab_size
    terms = mine.reshape(chips, vocab_size, share, pair).transpose(1, 0, 2, 3)
    terms = terms.reshape(vocab_size, chips * share, pair)
    terms = jnp.concatenate([terms, jnp.broadcast_to(target_sum, (vocab_size, 8, pair))], axis=1)
    terms = jnp.sum(exchange(terms, VOCAB), axis=0)
    total = (terms[: chips * share] * factor).astype(BF16).reshape(chips, share, pair)
    total = flip(total, core, 2)
    parts = jnp.stack(three(terms[chips * share]) + [jnp.zeros((pair,), BF16)], axis=0)
    parts = jnp.broadcast_to(parts, (chips,) + parts.shape)
    mine = exchange(jnp.concatenate([total, parts], axis=1), CHIPS)
    sums = jnp.sum(mine[:, share:, 0].astype(F32))
    mine = mine[:, :share].transpose(1, 0, 2).reshape(1, share, features)
    grad_hidden = exchange(
        jnp.broadcast_to(mine, (vocab_size, share, features)), VOCAB).reshape(tokens_own, features)

    loss = (norm_sum - sums) / count
    return grad_hidden, grad_head, loss


def solution(mesh):
    fine = Mesh(mesh.devices.reshape(2, RING, 2, 2, 4), ("yh", "z", "c", "yl", "x"))
    return jax.shard_map(
        on_device,
        mesh=fine,
        in_specs=(P(DP, None), P(VOCAB, DP), P(DP), P(DP), P()),
        out_specs=(P(DP, None), P(VOCAB, DP), P()),
        check_vma=False,
    )
```

```python
import functools

import jax
import jax.numpy as jnp
from jax import lax
from jax.experimental import pallas as pl
from jax.experimental.pallas import tpu as pltpu
from jax.sharding import Mesh, PartitionSpec as P

F32 = jnp.float32
BF16 = jnp.bfloat16
F16 = jnp.float16
DP = ("yh", "z", "c")
CHIPS = ("yh", "z")
VOCAB = ("yl", "x")
RING = 8
LANES = 128
PACKED = 160
SMEM = pl.BlockSpec(memory_space=pltpu.SMEM)
VMEM = pl.BlockSpec(memory_space=pltpu.VMEM)
PARAMS = pltpu.CompilerParams(vmem_limit_bytes=32 * 1024 * 1024)


def swap(value, axis):
    return lax.ppermute(value, axis, [(0, 1), (1, 0)])


def hop(value, step):
    return lax.ppermute(value, "z", [(i, (i + step) % RING) for i in range(RING)])


def dot(a, b, contract):
    return lax.dot_general(a, b, (contract, ((), ())), preferred_element_type=F32)


def exchange(value, axes):
    return lax.all_to_all(value, axes, split_axis=0, concat_axis=0, tiled=True)


def three(value):
    high = lax.reduce_precision(value, 8, 7)
    mid = lax.reduce_precision(value - high, 8, 7)
    return [part.astype(BF16) for part in (high, mid, value - high - mid)]


def split(value):
    high = value.astype(BF16)
    rest = value - high.astype(F32)
    mid = rest.astype(BF16)
    return high, mid, (rest - mid.astype(F32)).astype(BF16)


def flip(value, which, axis):
    first, second = jnp.split(value, 2, axis)
    return jnp.where(which == 0, value, jnp.concatenate([second, first], axis))


def outbox_kernel(hidden, targets, norm, out):
    tokens = hidden.shape[0]
    chips, _, wide = out.shape
    pair = wide - LANES
    eye = lax.broadcasted_iota(jnp.int32, (tokens, tokens), 0) == lax.broadcasted_iota(
        jnp.int32, (tokens, tokens), 1)
    code = jnp.sum(jnp.where(eye, targets[...] + 1, 0), axis=1, keepdims=True)
    column = jnp.sum(jnp.where(eye, norm[...], 0.0), axis=1, keepdims=True)
    values = [(code >> 8).astype(F32), (code & 255).astype(F32)]
    values += [part.astype(F32) for part in split(column)]
    lane = lax.broadcasted_iota(jnp.int32, (tokens, LANES), 1)
    facts = jnp.zeros((tokens, LANES), F32)
    for i, value in enumerate(values):
        facts = jnp.where(lane == i, value, facts)
    facts = facts.astype(BF16)
    for i in range(chips):
        out[i, :, :pair] = hidden[:, i * pair : (i + 1) * pair]
        out[i, :, pair:] = facts


def outbox(hidden, targets, log_norm, chips):
    tokens, features = hidden.shape
    return pl.pallas_call(
        outbox_kernel,
        out_shape=jax.ShapeDtypeStruct((chips, tokens, features // chips + LANES), BF16),
        in_specs=[VMEM] * 3,
        out_specs=VMEM,
        compiler_params=PARAMS,
        name="outbox",
    )(hidden, targets[None], log_norm[None])


def inbox_kernel(core, a, b, hid_a, hid_b, facts_a, facts_b, back, sums, *, shares, chips):
    span, wide = a.shape
    rows = hid_a.shape[0]
    pair = wide - LANES
    half = pair // 2
    tokens = span // chips
    share = tokens // shares
    r = lax.broadcasted_iota(jnp.int32, (span, span), 0)
    c = lax.broadcasted_iota(jnp.int32, (span, span), 1)
    before = (c <= r).astype(F32).astype(BF16)
    slot = lax.broadcasted_iota(jnp.int32, (span, rows), 1).astype(F32)
    counts, norms = [], []
    for x, hid, facts in ((a, hid_a, facts_a), (b, hid_b, facts_b)):
        own = x[:, pair:].astype(F32)
        code = own[:, 0:1] * 256.0 + own[:, 1:2]
        norm = own[:, 2:3] + own[:, 3:4] + own[:, 4:5]
        kept = jnp.where(code > 0.0, 1.0, 0.0)
        rank = dot(before, jnp.broadcast_to(kept, (span, LANES)).astype(BF16), ((1,), (0,)))
        place = jnp.where((rank[:, 0:1] - 1.0 == slot) & (kept > 0.0), 1.0, 0.0).astype(BF16)
        packed = dot(place, x[...], ((0,), (0,)))
        first, second = packed[:, :half], packed[:, half:pair]
        hid[:, :half] = jnp.where(core[0] == 0, first, second).astype(BF16)
        hid[:, half:] = jnp.where(core[0] == 0, second, first).astype(BF16)
        end = packed[:, pair:]
        lane = lax.broadcasted_iota(jnp.int32, (rows, LANES), 1)
        facts[...] = jnp.where(
            lane == 0, end[:, 0:1] * 256.0 + end[:, 1:2] - 1.0,
            jnp.where(lane == 1, end[:, 2:3] + end[:, 3:4] + end[:, 4:5], 0.0))
        counts.append(jnp.sum(kept, axis=0, keepdims=True))
        norms.append(jnp.sum(kept * norm, axis=0, keepdims=True))
        if x is a:
            w, rest = r // (chips * share), r % (chips * share)
            source = rest // share * tokens + w * share + rest % share
            order = jnp.where(c == source, 1.0, 0.0).astype(BF16)
            back[...] = dot(order, place, ((1,), (0,))).astype(BF16)
    row = lax.broadcasted_iota(jnp.int32, (8, LANES), 0)
    sums[...] = jnp.where(
        row == 0, counts[0] + counts[1],
        jnp.where(row == 1, norms[0] + norms[1], jnp.maximum(counts[0], counts[1])))


def inbox(core, a, b, rows, shares, chips):
    span, wide = a.shape
    pair = wide - LANES
    return pl.pallas_call(
        functools.partial(inbox_kernel, shares=shares, chips=chips),
        out_shape=(
            jax.ShapeDtypeStruct((rows, pair), BF16), jax.ShapeDtypeStruct((rows, pair), BF16),
            jax.ShapeDtypeStruct((rows, LANES), F32), jax.ShapeDtypeStruct((rows, LANES), F32),
            jax.ShapeDtypeStruct((span, rows), BF16), jax.ShapeDtypeStruct((8, LANES), F32)),
        in_specs=[SMEM, VMEM, VMEM],
        out_specs=(VMEM,) * 6,
        compiler_params=PARAMS,
        name="inbox",
    )(core, a, b)


def terms_kernel(mine, other, back, loss, out):
    half = mine.shape[1] // 2
    own = back[...]
    for at, seen in ((0, half), (half, 0)):
        total = mine[:, at : at + half] + other[:, seen : seen + half]
        full = sum(dot(own, part, ((1,), (0,))) for part in split(total))
        block = full.shape[0] // out.shape[0]
        for w in range(out.shape[0]):
            out[w, :block, at : at + half] = full[w * block : (w + 1) * block]
            out[w, block:, at : at + half] = jnp.full((8, half), loss[0], F32)


def terms_of(mine, other, back, loss, shares):
    return pl.pallas_call(
        terms_kernel,
        out_shape=jax.ShapeDtypeStruct(
            (shares, back.shape[0] // shares + 8, mine.shape[1]), F32),
        in_specs=[VMEM, VMEM, VMEM, SMEM],
        out_specs=VMEM,
        compiler_params=PARAMS,
        name="terms",
    )(mine, other, back, loss.reshape(1))


def head_rows(pieces, hid, factor, core, z, rows, width):
    half = rows // 2
    chunk = half // RING

    def kernel(places, scale, *refs):
        pieces, (hid_a, hid_b, own, give, held, sems) = refs[: 2 * RING], refs[2 * RING :]
        copies = [None, None]
        for d in range(RING):
            slot = d % 2
            if copies[slot] is not None:
                for copy in copies[slot]:
                    copy.wait()
            made = dot(pieces[d][...], hid_a[...], ((0,), (0,)))
            made += dot(pieces[RING + d][...], hid_b[...], ((0,), (0,)))
            held[slot] = (made * scale[0]).astype(BF16)
            at = pl.multiple_of(places[d], chunk)
            copies[slot] = (
                pltpu.make_async_copy(
                    held.at[slot, :, pl.ds(0, width)],
                    own.at[pl.ds(pl.multiple_of(places[RING] + at, chunk), chunk)],
                    sems.at[slot, 0]),
                pltpu.make_async_copy(
                    held.at[slot, :, pl.ds(width, width)],
                    give.at[pl.ds(at, chunk)], sems.at[slot, 1]),
            )
            for copy in copies[slot]:
                copy.start()
        for pair in copies:
            for copy in pair:
                copy.wait()

    order = lax.rem(z + jnp.arange(RING, dtype=jnp.int32), RING) * chunk
    places = jnp.concatenate([order, (core * half).reshape(1).astype(jnp.int32)])
    return pl.pallas_call(
        kernel,
        out_shape=(
            jax.ShapeDtypeStruct((rows, width), BF16), jax.ShapeDtypeStruct((half, width), BF16)),
        in_specs=[SMEM, SMEM] + [VMEM] * (2 * RING + 2),
        out_specs=(pl.BlockSpec(memory_space=pl.ANY), pl.BlockSpec(memory_space=pl.ANY)),
        scratch_shapes=[
            pltpu.VMEM((2, chunk, 2 * width), BF16),
            pltpu.SemaphoreType.DMA((2, 2)),
        ],
        compiler_params=PARAMS,
        cost_estimate=pl.CostEstimate(
            flops=4 * hid[0].shape[0] * half * 2 * width, bytes_accessed=9 << 20, transcendentals=0),
        name="head_rows",
    )(places, factor.reshape(1), *pieces, *hid)


def passes(box, head, wide, loss_scale, tokens_own):
    hid, facts, back, sums = box[:2], box[2:4], box[4], box[5]
    rows, width = head.shape
    half = rows // 2
    chunk = half // RING
    pair = 2 * width
    chips = lax.axis_size(CHIPS)
    vocab_size = lax.axis_size(VOCAB)
    core = lax.axis_index("c")
    yh = lax.axis_index("yh")
    z = lax.axis_index("z")
    share = tokens_own // vocab_size
    count, norm_sum = sums[0, 0], sums[1, 0]
    factor = loss_scale / count

    def place(distance):
        return lax.rem(z + distance + RING, RING) * chunk

    def head_chunk(distance):
        return lax.dynamic_slice_in_dim(wide, place(distance), chunk, 0)

    grad, target_sum = [], 0.0
    first = lax.axis_index(VOCAB) * rows + core * half + z * chunk
    ids = (first + jnp.arange(chunk, dtype=jnp.int32)).astype(F32)
    for s in range(2):
        way = 1 if s == 0 else -1
        target, norm = facts[s][:, 0:1], facts[s][:, 1:2]
        total = None
        for direction, length in ((way, RING // 2), (-way, RING // 2 - 1)):
            arrived = None
            for distance in range(length, 0, -1):
                term = dot(hid[s], head_chunk(direction * distance), ((1,), (1,)))
                if arrived is not None:
                    term = term + arrived.astype(F32)
                arrived = hop(term.astype(F16), direction)
            total = arrived.astype(F32) if total is None else total + arrived.astype(F32)
        total = total + dot(hid[s], head_chunk(0), ((1,), (1,)))
        logits = total + swap(total.astype(F16), "yh").astype(F32)
        onehot = ids[None, :] == target
        probs = jnp.exp(logits - norm)
        grad.append(jnp.where(target >= 0.0, probs - onehot.astype(F32), 0.0).astype(BF16))
        target_sum += jnp.sum(jnp.where(onehot, logits, 0.0))
    target_sum = jnp.where(yh == 0, target_sum, 0.0)
    target_sum = target_sum + swap(target_sum, "c")

    pieces = {}
    hidden_grad = [None, None]
    for s in range(2):
        way = 1 if s == 0 else -1
        pieces[s, 0] = grad[s]
        for direction, length in ((way, RING // 2), (-way, RING // 2 - 1)):
            arrived = grad[s]
            for distance in range(1, length + 1):
                arrived = hop(arrived, direction)
                pieces[s, (-direction * distance) % RING] = arrived
        for distance in (0, 1, 7, 2, 6, 3, 5, 4):
            term = dot(pieces[s, distance], head_chunk(distance), ((1,), (0,)))
            hidden_grad[s] = term if hidden_grad[s] is None else hidden_grad[s] + term

    grad_head, give = head_rows(
        [pieces[s, d] for s in range(2) for d in range(RING)], hid, factor, core, z, rows, width)
    grad_head = lax.dynamic_update_slice_in_dim(grad_head, swap(give, "c"), (1 - core) * half, 0)

    terms = terms_of(hidden_grad[0], swap(hidden_grad[1], "c"), back, target_sum, vocab_size)
    terms = jnp.sum(exchange(terms, VOCAB), axis=0)
    total = (terms[: chips * share] * factor).astype(BF16).reshape(chips, share, pair)
    total = flip(total, core, 2)
    parts = jnp.stack(three(terms[chips * share]) + [jnp.zeros((pair,), BF16)], axis=0)
    parts = jnp.broadcast_to(parts, (chips,) + parts.shape)
    mine = exchange(jnp.concatenate([total, parts], axis=1), CHIPS)
    sums = jnp.sum(mine[:, share:, 0].astype(F32))
    mine = mine[:, :share].transpose(1, 0, 2).reshape(1, share, chips * pair)
    grad_hidden = exchange(
        jnp.broadcast_to(mine, (vocab_size, share, chips * pair)), VOCAB)
    return grad_hidden.reshape(tokens_own, chips * pair), grad_head, (norm_sum - sums) / count


def on_device(hidden, head, targets, log_norm, loss_scale):
    half = head.shape[0] // 2
    tokens_own = hidden.shape[0]
    chips = lax.axis_size(CHIPS)
    shares = lax.axis_size(VOCAB)
    core = lax.axis_index("c")
    span = chips * tokens_own

    got = exchange(outbox(hidden, targets, log_norm, chips), CHIPS)
    a = got.reshape(span, -1)
    b = swap(got, "c").reshape(span, -1)

    own = lax.dynamic_slice_in_dim(head, core * half, half, 0)
    away = lax.dynamic_slice_in_dim(head, (1 - core) * half, half, 0)
    wide = lax.optimization_barrier(jnp.concatenate([own, swap(away, "c")], axis=1))

    where = core.reshape(1).astype(jnp.int32)
    box = inbox(where, a, b, PACKED, shares, chips)
    return lax.cond(
        box[5][2, 0] <= PACKED,
        lambda: passes(box, head, wide, loss_scale, tokens_own),
        lambda: passes(
            inbox(where, a, b, span, shares, chips), head, wide, loss_scale, tokens_own))


def solution(mesh):
    fine = Mesh(mesh.devices.reshape(2, RING, 2, 2, 4), ("yh", "z", "c", "yl", "x"))
    return jax.shard_map(
        on_device,
        mesh=fine,
        in_specs=(P(DP, None), P(VOCAB, DP), P(DP), P(DP), P()),
        out_specs=(P(DP, None), P(VOCAB, DP), P()),
        check_vma=False,
    )
```

```python
import functools

import jax
import jax.numpy as jnp
from jax import lax
from jax.experimental import pallas as pl
from jax.experimental.pallas import tpu as pltpu
from jax.sharding import Mesh, PartitionSpec as P

F32 = jnp.float32
BF16 = jnp.bfloat16
F16 = jnp.float16
DP = ("yh", "z", "c")
CHIPS = ("yh", "z")
VOCAB = ("yl", "x")
RING = 8
LANES = 128
PACKED = 160
SMEM = pl.BlockSpec(memory_space=pltpu.SMEM)
VMEM = pl.BlockSpec(memory_space=pltpu.VMEM)
PARAMS = pltpu.CompilerParams(vmem_limit_bytes=32 * 1024 * 1024)


def swap(value, axis):
    return lax.ppermute(value, axis, [(0, 1), (1, 0)])


def hop(value, step):
    return lax.ppermute(value, "z", [(i, (i + step) % RING) for i in range(RING)])


def dot(a, b, contract):
    return lax.dot_general(a, b, (contract, ((), ())), preferred_element_type=F32)


def exchange(value, axes):
    return lax.all_to_all(value, axes, split_axis=0, concat_axis=0, tiled=True)


def three(value):
    high = lax.reduce_precision(value, 8, 7)
    mid = lax.reduce_precision(value - high, 8, 7)
    return [part.astype(BF16) for part in (high, mid, value - high - mid)]


def split(value):
    high = value.astype(BF16)
    rest = value - high.astype(F32)
    mid = rest.astype(BF16)
    return high, mid, (rest - mid.astype(F32)).astype(BF16)


def flip(value, which, axis):
    first, second = jnp.split(value, 2, axis)
    return jnp.where(which == 0, value, jnp.concatenate([second, first], axis))


def outbox_kernel(hidden, targets, norm, out):
    tokens = hidden.shape[0]
    chips, _, wide = out.shape
    pair = wide - LANES
    eye = lax.broadcasted_iota(jnp.int32, (tokens, tokens), 0) == lax.broadcasted_iota(
        jnp.int32, (tokens, tokens), 1)
    code = jnp.sum(jnp.where(eye, targets[...] + 1, 0), axis=1, keepdims=True)
    column = jnp.sum(jnp.where(eye, norm[...], 0.0), axis=1, keepdims=True)
    values = [(code >> 8).astype(F32), (code & 255).astype(F32)]
    values += [part.astype(F32) for part in split(column)]
    lane = lax.broadcasted_iota(jnp.int32, (tokens, LANES), 1)
    facts = jnp.zeros((tokens, LANES), F32)
    for i, value in enumerate(values):
        facts = jnp.where(lane == i, value, facts)
    facts = facts.astype(BF16)
    for i in range(chips):
        out[i, :, :pair] = hidden[:, i * pair : (i + 1) * pair]
        out[i, :, pair:] = facts


def outbox(hidden, targets, log_norm, chips):
    tokens, features = hidden.shape
    return pl.pallas_call(
        outbox_kernel,
        out_shape=jax.ShapeDtypeStruct((chips, tokens, features // chips + LANES), BF16),
        in_specs=[VMEM] * 3,
        out_specs=VMEM,
        compiler_params=PARAMS,
        name="outbox",
    )(hidden, targets[None], log_norm[None])


def inbox_kernel(core, a, b, hid_a, hid_b, facts_a, facts_b, back, sums, *, shares, chips):
    span, wide = a.shape
    rows = hid_a.shape[0]
    pair = wide - LANES
    half = pair // 2
    tokens = span // chips
    share = tokens // shares
    r = lax.broadcasted_iota(jnp.int32, (span, span), 0)
    c = lax.broadcasted_iota(jnp.int32, (span, span), 1)
    before = (c <= r).astype(F32).astype(BF16)
    slot = lax.broadcasted_iota(jnp.int32, (span, rows), 1).astype(F32)
    counts, norms = [], []
    for x, hid, facts in ((a, hid_a, facts_a), (b, hid_b, facts_b)):
        own = x[:, pair:].astype(F32)
        code = own[:, 0:1] * 256.0 + own[:, 1:2]
        norm = own[:, 2:3] + own[:, 3:4] + own[:, 4:5]
        kept = jnp.where(code > 0.0, 1.0, 0.0)
        rank = dot(before, jnp.broadcast_to(kept, (span, LANES)).astype(BF16), ((1,), (0,)))
        place = jnp.where((rank[:, 0:1] - 1.0 == slot) & (kept > 0.0), 1.0, 0.0).astype(BF16)
        packed = dot(place, x[...], ((0,), (0,)))
        first, second = packed[:, :half], packed[:, half:pair]
        hid[:, :half] = jnp.where(core[0] == 0, first, second).astype(BF16)
        hid[:, half:] = jnp.where(core[0] == 0, second, first).astype(BF16)
        end = packed[:, pair:]
        lane = lax.broadcasted_iota(jnp.int32, (rows, LANES), 1)
        facts[...] = jnp.where(
            lane == 0, end[:, 0:1] * 256.0 + end[:, 1:2] - 1.0,
            jnp.where(lane == 1, end[:, 2:3] + end[:, 3:4] + end[:, 4:5], 0.0))
        counts.append(jnp.sum(kept, axis=0, keepdims=True))
        norms.append(jnp.sum(kept * norm, axis=0, keepdims=True))
        if x is a:
            w, rest = r // (chips * share), r % (chips * share)
            source = rest // share * tokens + w * share + rest % share
            order = jnp.where(c == source, 1.0, 0.0).astype(BF16)
            back[...] = dot(order, place, ((1,), (0,))).astype(BF16)
    row = lax.broadcasted_iota(jnp.int32, (8, LANES), 0)
    sums[...] = jnp.where(
        row == 0, counts[0] + counts[1],
        jnp.where(row == 1, norms[0] + norms[1], jnp.maximum(counts[0], counts[1])))


def inbox(core, a, b, rows, shares, chips):
    span, wide = a.shape
    pair = wide - LANES
    return pl.pallas_call(
        functools.partial(inbox_kernel, shares=shares, chips=chips),
        out_shape=(
            jax.ShapeDtypeStruct((rows, pair), BF16), jax.ShapeDtypeStruct((rows, pair), BF16),
            jax.ShapeDtypeStruct((rows, LANES), F32), jax.ShapeDtypeStruct((rows, LANES), F32),
            jax.ShapeDtypeStruct((span, rows), BF16), jax.ShapeDtypeStruct((8, LANES), F32)),
        in_specs=[SMEM, VMEM, VMEM],
        out_specs=(VMEM,) * 6,
        compiler_params=PARAMS,
        name="inbox",
    )(core, a, b)


def terms_kernel(mine, other, back, loss, out):
    half = mine.shape[1] // 2
    own = back[...]
    for at, seen in ((0, half), (half, 0)):
        total = mine[:, at : at + half] + other[:, seen : seen + half]
        full = sum(dot(own, part, ((1,), (0,))) for part in split(total))
        block = full.shape[0] // out.shape[0]
        for w in range(out.shape[0]):
            out[w, :block, at : at + half] = full[w * block : (w + 1) * block]
            out[w, block:, at : at + half] = jnp.full((8, half), loss[0], F32)


def terms_of(mine, other, back, loss, shares):
    return pl.pallas_call(
        terms_kernel,
        out_shape=jax.ShapeDtypeStruct(
            (shares, back.shape[0] // shares + 8, mine.shape[1]), F32),
        in_specs=[VMEM, VMEM, VMEM, SMEM],
        out_specs=VMEM,
        compiler_params=PARAMS,
        name="terms",
    )(mine, other, back, loss.reshape(1))


def head_rows(pieces, hid, factor, core, z, rows, width):
    half = rows // 2
    chunk = half // RING

    def kernel(places, scale, *refs):
        pieces, (hid_a, hid_b, own, give, held, sems) = refs[: 2 * RING], refs[2 * RING :]
        copies = [None, None]
        for d in range(RING):
            slot = d % 2
            if copies[slot] is not None:
                for copy in copies[slot]:
                    copy.wait()
            made = dot(pieces[d][...], hid_a[...], ((0,), (0,)))
            made += dot(pieces[RING + d][...], hid_b[...], ((0,), (0,)))
            held[slot] = (made * scale[0]).astype(BF16)
            at = pl.multiple_of(places[d], chunk)
            copies[slot] = (
                pltpu.make_async_copy(
                    held.at[slot, :, pl.ds(0, width)],
                    own.at[pl.ds(pl.multiple_of(places[RING] + at, chunk), chunk)],
                    sems.at[slot, 0]),
                pltpu.make_async_copy(
                    held.at[slot, :, pl.ds(width, width)],
                    give.at[pl.ds(at, chunk)], sems.at[slot, 1]),
            )
            for copy in copies[slot]:
                copy.start()
        for pair in copies:
            for copy in pair:
                copy.wait()

    order = lax.rem(z + jnp.arange(RING, dtype=jnp.int32), RING) * chunk
    places = jnp.concatenate([order, (core * half).reshape(1).astype(jnp.int32)])
    return pl.pallas_call(
        kernel,
        out_shape=(
            jax.ShapeDtypeStruct((rows, width), BF16), jax.ShapeDtypeStruct((half, width), BF16)),
        in_specs=[SMEM, SMEM] + [VMEM] * (2 * RING + 2),
        out_specs=(pl.BlockSpec(memory_space=pl.ANY), pl.BlockSpec(memory_space=pl.ANY)),
        scratch_shapes=[
            pltpu.VMEM((2, chunk, 2 * width), BF16),
            pltpu.SemaphoreType.DMA((2, 2)),
        ],
        compiler_params=PARAMS,
        cost_estimate=pl.CostEstimate(
            flops=4 * hid[0].shape[0] * half * 2 * width, bytes_accessed=9 << 20, transcendentals=0),
        name="head_rows",
    )(places, factor.reshape(1), *pieces, *hid)


def passes(box, head, wide, loss_scale, tokens_own):
    hid, facts, back, sums = box[:2], box[2:4], box[4], box[5]
    rows, width = head.shape
    half = rows // 2
    chunk = half // RING
    pair = 2 * width
    chips = lax.axis_size(CHIPS)
    vocab_size = lax.axis_size(VOCAB)
    core = lax.axis_index("c")
    yh = lax.axis_index("yh")
    z = lax.axis_index("z")
    share = tokens_own // vocab_size
    count, norm_sum = sums[0, 0], sums[1, 0]
    factor = loss_scale / count

    def place(distance):
        return lax.rem(z + distance + RING, RING) * chunk

    chunks = [
        lax.optimization_barrier(lax.dynamic_slice_in_dim(wide, place(d), chunk, 0))
        for d in range(RING)]

    def head_chunk(distance):
        return chunks[distance % RING]

    grad, target_sum = [], 0.0
    first = lax.axis_index(VOCAB) * rows + core * half + z * chunk
    ids = (first + jnp.arange(chunk, dtype=jnp.int32)).astype(F32)
    for s in range(2):
        way = 1 if s == 0 else -1
        target, norm = facts[s][:, 0:1], facts[s][:, 1:2]
        total = None
        for direction, length in ((way, RING // 2), (-way, RING // 2 - 1)):
            arrived = None
            for distance in range(length, 0, -1):
                term = dot(hid[s], head_chunk(direction * distance), ((1,), (1,)))
                if arrived is not None:
                    term = term + arrived.astype(F32)
                arrived = hop(term.astype(F16), direction)
            total = arrived.astype(F32) if total is None else total + arrived.astype(F32)
        total = total + dot(hid[s], head_chunk(0), ((1,), (1,)))
        logits = total + swap(total.astype(F16), "yh").astype(F32)
        onehot = ids[None, :] == target
        probs = jnp.exp(logits - norm)
        grad.append(jnp.where(target >= 0.0, probs - onehot.astype(F32), 0.0).astype(BF16))
        target_sum += jnp.sum(jnp.where(onehot, logits, 0.0))
    target_sum = jnp.where(yh == 0, target_sum, 0.0)
    target_sum = target_sum + swap(target_sum, "c")

    pieces = {}
    hidden_grad = [None, None]
    for s in range(2):
        way = 1 if s == 0 else -1
        pieces[s, 0] = grad[s]
        for direction, length in ((way, RING // 2), (-way, RING // 2 - 1)):
            arrived = grad[s]
            for distance in range(1, length + 1):
                arrived = hop(arrived, direction)
                pieces[s, (-direction * distance) % RING] = arrived
        for distance in (0, 1, 7, 2, 6, 3, 5, 4):
            term = dot(pieces[s, distance], head_chunk(distance), ((1,), (0,)))
            hidden_grad[s] = term if hidden_grad[s] is None else hidden_grad[s] + term

    grad_head, give = head_rows(
        [pieces[s, d] for s in range(2) for d in range(RING)], hid, factor, core, z, rows, width)
    grad_head = lax.dynamic_update_slice_in_dim(grad_head, swap(give, "c"), (1 - core) * half, 0)

    terms = terms_of(hidden_grad[0], swap(hidden_grad[1], "c"), back, target_sum, vocab_size)
    terms = jnp.sum(exchange(terms, VOCAB), axis=0)
    total = (terms[: chips * share] * factor).astype(BF16).reshape(chips, share, pair)
    total = flip(total, core, 2)
    parts = jnp.stack(three(terms[chips * share]) + [jnp.zeros((pair,), BF16)], axis=0)
    parts = jnp.broadcast_to(parts, (chips,) + parts.shape)
    mine = exchange(jnp.concatenate([total, parts], axis=1), CHIPS)
    sums = jnp.sum(mine[:, share:, 0].astype(F32))
    mine = mine[:, :share].transpose(1, 0, 2).reshape(1, share, chips * pair)
    grad_hidden = exchange(
        jnp.broadcast_to(mine, (vocab_size, share, chips * pair)), VOCAB)
    return grad_hidden.reshape(tokens_own, chips * pair), grad_head, (norm_sum - sums) / count


def on_device(hidden, head, targets, log_norm, loss_scale):
    half = head.shape[0] // 2
    tokens_own = hidden.shape[0]
    chips = lax.axis_size(CHIPS)
    shares = lax.axis_size(VOCAB)
    core = lax.axis_index("c")
    span = chips * tokens_own

    got = exchange(outbox(hidden, targets, log_norm, chips), CHIPS)
    a = got.reshape(span, -1)
    b = swap(got, "c").reshape(span, -1)

    own = lax.dynamic_slice_in_dim(head, core * half, half, 0)
    away = lax.dynamic_slice_in_dim(head, (1 - core) * half, half, 0)
    wide = lax.optimization_barrier(jnp.concatenate([own, swap(away, "c")], axis=1))

    where = core.reshape(1).astype(jnp.int32)
    box = inbox(where, a, b, PACKED, shares, chips)
    outputs = passes(box, head, wide, loss_scale, tokens_own)

    def again(state):
        full = inbox(where, a, b, span, shares, chips)
        return (jnp.bool_(False),) + passes(full, head, wide, loss_scale, tokens_own)

    state = lax.while_loop(lambda state: state[0], again, (box[5][2, 0] > PACKED,) + outputs)
    return state[1:]


def solution(mesh):
    fine = Mesh(mesh.devices.reshape(2, RING, 2, 2, 4), ("yh", "z", "c", "yl", "x"))
    return jax.shard_map(
        on_device,
        mesh=fine,
        in_specs=(P(DP, None), P(VOCAB, DP), P(DP), P(DP), P()),
        out_specs=(P(DP, None), P(VOCAB, DP), P()),
        check_vma=False,
    )
```

```python
import functools

import jax
import jax.numpy as jnp
from jax import lax
from jax.experimental import pallas as pl
from jax.experimental.pallas import tpu as pltpu
from jax.sharding import Mesh, PartitionSpec as P

F32 = jnp.float32
BF16 = jnp.bfloat16
F16 = jnp.float16
DP = ("yh", "z", "c")
CHIPS = ("yh", "z")
VOCAB = ("yl", "x")
RING = 8
LANES = 128
PACKED = 160
SMEM = pl.BlockSpec(memory_space=pltpu.SMEM)
VMEM = pl.BlockSpec(memory_space=pltpu.VMEM)
PARAMS = pltpu.CompilerParams(vmem_limit_bytes=32 * 1024 * 1024)


def swap(value, axis):
    return lax.ppermute(value, axis, [(0, 1), (1, 0)])


def hop(value, step):
    return lax.ppermute(value, "z", [(i, (i + step) % RING) for i in range(RING)])


def dot(a, b, contract):
    return lax.dot_general(a, b, (contract, ((), ())), preferred_element_type=F32)


def exchange(value, axes):
    return lax.all_to_all(value, axes, split_axis=0, concat_axis=0, tiled=True)


def split(value):
    high = value.astype(BF16)
    rest = value - high.astype(F32)
    mid = rest.astype(BF16)
    return high, mid, (rest - mid.astype(F32)).astype(BF16)


def outbox_kernel(hidden, targets, norm, out):
    tokens = hidden.shape[0]
    chips, _, wide = out.shape
    pair = wide - LANES
    eye = lax.broadcasted_iota(jnp.int32, (tokens, tokens), 0) == lax.broadcasted_iota(
        jnp.int32, (tokens, tokens), 1)
    code = jnp.sum(jnp.where(eye, targets[...] + 1, 0), axis=1, keepdims=True)
    column = jnp.sum(jnp.where(eye, norm[...], 0.0), axis=1, keepdims=True)
    values = [(code >> 8).astype(F32), (code & 255).astype(F32)]
    values += [part.astype(F32) for part in split(column)]
    lane = lax.broadcasted_iota(jnp.int32, (tokens, LANES), 1)
    facts = jnp.zeros((tokens, LANES), F32)
    for i, value in enumerate(values):
        facts = jnp.where(lane == i, value, facts)
    facts = facts.astype(BF16)
    for i in range(chips):
        out[i, :, :pair] = hidden[:, i * pair : (i + 1) * pair]
        out[i, :, pair:] = facts


def outbox(hidden, targets, log_norm, chips):
    tokens, features = hidden.shape
    return pl.pallas_call(
        outbox_kernel,
        out_shape=jax.ShapeDtypeStruct((chips, tokens, features // chips + LANES), BF16),
        in_specs=[VMEM] * 3,
        out_specs=VMEM,
        compiler_params=PARAMS,
        name="outbox",
    )(hidden, targets[None], log_norm[None])


def inbox_kernel(core, a, b, hid_a, hid_b, facts_a, facts_b, back, sums, *, shares, chips):
    span, wide = a.shape
    rows = hid_a.shape[0]
    pair = wide - LANES
    half = pair // 2
    tokens = span // chips
    share = tokens // shares
    r = lax.broadcasted_iota(jnp.int32, (span, span), 0)
    c = lax.broadcasted_iota(jnp.int32, (span, span), 1)
    before = (c <= r).astype(F32).astype(BF16)
    slot = lax.broadcasted_iota(jnp.int32, (span, rows), 1).astype(F32)
    counts, norms = [], []
    for x, hid, facts in ((a, hid_a, facts_a), (b, hid_b, facts_b)):
        own = x[:, pair:].astype(F32)
        code = own[:, 0:1] * 256.0 + own[:, 1:2]
        norm = own[:, 2:3] + own[:, 3:4] + own[:, 4:5]
        kept = jnp.where(code > 0.0, 1.0, 0.0)
        rank = dot(before, jnp.broadcast_to(kept, (span, LANES)).astype(BF16), ((1,), (0,)))
        place = jnp.where((rank[:, 0:1] - 1.0 == slot) & (kept > 0.0), 1.0, 0.0).astype(BF16)
        packed = dot(place, x[...], ((0,), (0,)))
        first, second = packed[:, :half], packed[:, half:pair]
        hid[:, :half] = jnp.where(core[0] == 0, first, second).astype(BF16)
        hid[:, half:] = jnp.where(core[0] == 0, second, first).astype(BF16)
        end = packed[:, pair:]
        lane = lax.broadcasted_iota(jnp.int32, (rows, LANES), 1)
        facts[...] = jnp.where(
            lane == 0, end[:, 0:1] * 256.0 + end[:, 1:2] - 1.0,
            jnp.where(lane == 1, end[:, 2:3] + end[:, 3:4] + end[:, 4:5], 0.0))
        counts.append(jnp.sum(kept, axis=0, keepdims=True))
        norms.append(jnp.sum(kept * norm, axis=0, keepdims=True))
        if x is a:
            i, rest = r // (chips * shares), r % (chips * shares)
            source = rest // shares * tokens + rest % shares * share + i
            order = jnp.where(c == source, 1.0, 0.0).astype(BF16)
            back[...] = dot(order, place, ((1,), (0,))).astype(BF16)
    row = lax.broadcasted_iota(jnp.int32, (8, LANES), 0)
    sums[...] = jnp.where(
        row == 0, counts[0] + counts[1],
        jnp.where(row == 1, norms[0] + norms[1], jnp.maximum(counts[0], counts[1])))


def inbox(core, a, b, rows, shares, chips):
    span, wide = a.shape
    pair = wide - LANES
    return pl.pallas_call(
        functools.partial(inbox_kernel, shares=shares, chips=chips),
        out_shape=(
            jax.ShapeDtypeStruct((rows, pair), BF16), jax.ShapeDtypeStruct((rows, pair), BF16),
            jax.ShapeDtypeStruct((rows, LANES), F32), jax.ShapeDtypeStruct((rows, LANES), F32),
            jax.ShapeDtypeStruct((span, rows), BF16), jax.ShapeDtypeStruct((8, LANES), F32)),
        in_specs=[SMEM, VMEM, VMEM],
        out_specs=(VMEM,) * 6,
        compiler_params=PARAMS,
        name="inbox",
    )(core, a, b)


def grad_kernel(first, logits, facts, out):
    rows, chunk = logits.shape
    value = logits[...]
    target, norm = facts[:, 0:1], facts[:, 1:2]
    ids = lax.broadcasted_iota(jnp.int32, (rows, chunk), 1) + first[0]
    onehot = ids.astype(F32) == target
    probs = jnp.exp(value - norm)
    grad = jnp.where(target >= 0.0, probs - jnp.where(onehot, 1.0, 0.0), 0.0)
    picked = jnp.sum(jnp.where(onehot, value, 0.0), axis=1, keepdims=True)
    picked = jnp.sum(picked, axis=0, keepdims=True)
    lane = lax.broadcasted_iota(jnp.int32, (1, chunk), 1)
    last = jnp.zeros((1, chunk), F32)
    for i, part in enumerate(split(picked)):
        last = jnp.where(lane == i, part.astype(F32), last)
    row = lax.broadcasted_iota(jnp.int32, (rows, chunk), 0)
    out[...] = jnp.where(row == rows - 1, last, grad).astype(BF16)


def grad_of(first, logits, facts):
    return pl.pallas_call(
        grad_kernel,
        out_shape=jax.ShapeDtypeStruct(logits.shape, BF16),
        in_specs=[SMEM, VMEM, VMEM],
        out_specs=VMEM,
        compiler_params=PARAMS,
        name="grad",
    )(first, logits, facts)


def hidden_rows(earlier, pieces, wide, places):
    count = len(pieces) // 2
    rows, chunk = pieces[0].shape
    pair = wide.shape[1]

    def kernel(places, wide, *refs):
        pieces, before = refs[: 2 * count], refs[2 * count : 2 * count + len(earlier)]
        out_a, out_b, held, sems = refs[2 * count + len(earlier) :]
        copies = []
        for d in range(count):
            at = pl.multiple_of(places[d], chunk)
            copies.append(pltpu.make_async_copy(
                wide.at[pl.ds(at, chunk)], held.at[d], sems.at[d]))
            copies[d].start()
        total = [ref[...] for ref in before]
        picked = total[1][rows - 1 :, 0:1] if total else jnp.zeros((1, 1), F32)
        row = lax.broadcasted_iota(jnp.int32, (16, LANES), 0)
        lane = lax.broadcasted_iota(jnp.int32, (16, LANES), 1)
        for d in range(count):
            copies[d].wait()
            for s in range(2):
                piece = pieces[s * count + d]
                term = dot(piece[...], held[d], ((1,), (0,)))
                total = total + [term] if len(total) < 2 else [
                    t + term if i == s else t for i, t in enumerate(total)]
                end = piece[rows - 16 :, :LANES].astype(F32)
                end = jnp.where((row == 15) & (lane < 3), end, 0.0)
                picked += jnp.sum(jnp.sum(end, axis=1, keepdims=True), axis=0, keepdims=True)
        out_a[...] = total[0]
        last = lax.broadcasted_iota(jnp.int32, (rows, pair), 0) == rows - 1
        out_b[...] = jnp.where(last, picked, total[1])

    return pl.pallas_call(
        kernel,
        out_shape=(jax.ShapeDtypeStruct((rows, pair), F32),) * 2,
        in_specs=[SMEM, pl.BlockSpec(memory_space=pl.ANY)] + [VMEM] * (2 * count + len(earlier)),
        out_specs=(VMEM, VMEM),
        scratch_shapes=[
            pltpu.VMEM((count, chunk, pair), BF16), pltpu.SemaphoreType.DMA((count,))],
        compiler_params=PARAMS,
        cost_estimate=pl.CostEstimate(
            flops=4 * rows * chunk * pair * count, bytes_accessed=count << 20, transcendentals=0),
        name="hidden_rows",
    )(places, wide, *pieces, *earlier)


def terms_kernel(core, mine, own_b, other, back, out, picked):
    rows, pair = mine.shape
    half = pair // 2
    own = back[...]
    share = 8 // (pair // LANES)
    full = []
    for at, seen in ((0, half), (half, 0)):
        total = mine[:, at : at + half] + other[:, seen : seen + half]
        full.append(sum(dot(own, part, ((1,), (0,))) for part in split(total)))
    natural = (jnp.where(core[0] == 0, full[0], full[1]), jnp.where(core[0] == 0, full[1], full[0]))
    blocks = own.shape[0] // share
    tiles = pair // LANES
    for i in range(share):
        for j in range(tiles):
            side = natural[j * LANES // half]
            at = j * LANES % half
            out[pl.ds(i * tiles + j, blocks, stride=share * tiles), :] = side[
                i * blocks : (i + 1) * blocks, at : at + LANES]
    picked[...] = jnp.broadcast_to(
        own_b[rows - 1 :, :LANES] + other[rows - 1 :, :LANES], picked.shape)


def terms_of(core, mine, own_b, other, back):
    span, pair = back.shape[0], mine.shape[1]
    return pl.pallas_call(
        terms_kernel,
        out_shape=(
            jax.ShapeDtypeStruct((span * pair // LANES, LANES), F32),
            jax.ShapeDtypeStruct((8, LANES), F32)),
        in_specs=[SMEM] + [VMEM] * 4,
        out_specs=(VMEM, VMEM),
        compiler_params=PARAMS,
        name="terms",
    )(core, mine, own_b, other, back)


def collect_kernel(scale, terms, picked, out):
    chips = terms.shape[0] // 64
    total = jnp.sum(terms[...].reshape(chips, 8, 8, LANES), axis=1).reshape(chips * 8, LANES)
    value = (total * scale[0]).astype(BF16)
    row = lax.broadcasted_iota(jnp.int32, (16, LANES), 0)
    parts = jnp.zeros((16, LANES), F32)
    for i, part in enumerate(split(picked[0:1, :])):
        parts = jnp.where(row == i, part.astype(F32), parts)
    for w in range(out.shape[0]):
        out[w, : chips * 8] = value
        out[w, chips * 8 :] = parts.astype(BF16)


def collect(factor, terms, picked, shares, chips):
    return pl.pallas_call(
        collect_kernel,
        out_shape=jax.ShapeDtypeStruct((shares, chips * 8 + 16, LANES), BF16),
        in_specs=[SMEM, VMEM, VMEM],
        out_specs=VMEM,
        compiler_params=PARAMS,
        name="collect",
    )(factor.reshape(1), terms, picked)


def head_rows(pieces, hid, factor, core, order, rows, width):
    half = rows // 2
    chunk = half // RING

    def kernel(places, scale, *refs):
        pieces, (hid_a, hid_b, own, give, held, sems) = refs[: 2 * RING], refs[2 * RING :]
        copies = [None, None]
        for d in range(RING):
            slot = d % 2
            if copies[slot] is not None:
                for copy in copies[slot]:
                    copy.wait()
            made = dot(pieces[d][...], hid_a[...], ((0,), (0,)))
            made += dot(pieces[RING + d][...], hid_b[...], ((0,), (0,)))
            held[slot] = (made * scale[0]).astype(BF16)
            at = pl.multiple_of(places[d], chunk)
            copies[slot] = (
                pltpu.make_async_copy(
                    held.at[slot, :, pl.ds(0, width)],
                    own.at[pl.ds(pl.multiple_of(places[RING] + at, chunk), chunk)],
                    sems.at[slot, 0]),
                pltpu.make_async_copy(
                    held.at[slot, :, pl.ds(width, width)],
                    give.at[pl.ds(at, chunk)], sems.at[slot, 1]),
            )
            for copy in copies[slot]:
                copy.start()
        for pair in copies:
            for copy in pair:
                copy.wait()

    places = jnp.concatenate([order, (core * half).reshape(1).astype(jnp.int32)])
    return pl.pallas_call(
        kernel,
        out_shape=(
            jax.ShapeDtypeStruct((rows, width), BF16), jax.ShapeDtypeStruct((half, width), BF16)),
        in_specs=[SMEM, SMEM] + [VMEM] * (2 * RING + 2),
        out_specs=(pl.BlockSpec(memory_space=pl.ANY), pl.BlockSpec(memory_space=pl.ANY)),
        scratch_shapes=[
            pltpu.VMEM((2, chunk, 2 * width), BF16),
            pltpu.SemaphoreType.DMA((2, 2)),
        ],
        compiler_params=PARAMS,
        cost_estimate=pl.CostEstimate(
            flops=4 * hid[0].shape[0] * half * 2 * width, bytes_accessed=9 << 20, transcendentals=0),
        name="head_rows",
    )(places, factor.reshape(1), *pieces, *hid)


def passes(box, head, wide, chunks, loss_scale, tokens_own):
    hid, facts, back, sums = box[:2], box[2:4], box[4], box[5]
    rows, width = head.shape
    half = rows // 2
    chunk = half // RING
    pair = 2 * width
    chips = lax.axis_size(CHIPS)
    shares = lax.axis_size(VOCAB)
    core = lax.axis_index("c")
    z = lax.axis_index("z")
    share = tokens_own // shares
    count, norm_sum = sums[0, 0], sums[1, 0]
    factor = loss_scale / count
    where = core.reshape(1).astype(jnp.int32)
    first = (lax.axis_index(VOCAB) * rows + core * half + z * chunk).reshape(1).astype(jnp.int32)
    order = lax.rem(z + jnp.arange(RING, dtype=jnp.int32), RING) * chunk

    grad = []
    for s in range(2):
        way = 1 if s == 0 else -1
        total = None
        for direction, length in ((way, RING // 2), (-way, RING // 2 - 1)):
            arrived = None
            for distance in range(length, 0, -1):
                term = dot(hid[s], chunks[direction * distance % RING], ((1,), (1,)))
                if arrived is not None:
                    term = term + arrived.astype(F32)
                arrived = hop(term.astype(F16), direction)
            total = arrived.astype(F32) if total is None else total + arrived.astype(F32)
        total = total + dot(hid[s], chunks[0], ((1,), (1,)))
        logits = total + swap(total.astype(F16), "yh").astype(F32)
        grad.append(grad_of(first, logits, facts[s]))

    pieces = {}
    for s in range(2):
        way = 1 if s == 0 else -1
        pieces[s, 0] = grad[s]
        for direction, length in ((way, RING // 2), (-way, RING // 2 - 1)):
            arrived = grad[s]
            for distance in range(1, length + 1):
                arrived = hop(arrived, direction)
                pieces[s, (-direction * distance) % RING] = arrived

    hidden_grad = ()
    for batch in ((0, 1, 7, 2, 6), (3, 5, 4)):
        hidden_grad = hidden_rows(
            hidden_grad, [pieces[s, d] for s in range(2) for d in batch], wide,
            jnp.stack([order[d] for d in batch]))

    grad_head, give = head_rows(
        [pieces[s, d] for s in range(2) for d in range(RING)], hid, factor, core, order, rows, width)
    grad_head = lax.dynamic_update_slice_in_dim(grad_head, swap(give, "c"), (1 - core) * half, 0)

    other = swap(hidden_grad[1], "c")
    terms, picked = terms_of(where, hidden_grad[0], hidden_grad[1], other, back)
    terms = exchange(terms.reshape(chips * shares, 8, LANES), CHIPS + VOCAB)
    mine = collect(factor, terms.reshape(-1, LANES), picked, shares, chips)
    ends = exchange(mine, VOCAB)
    picked = jnp.sum(ends[:, chips * 8 : chips * 8 + 3, 0].astype(F32))
    tiles = pair // LANES
    ends = ends[:, : chips * 8].reshape(shares, chips, share, tiles * LANES)
    grad_hidden = ends.transpose(0, 2, 1, 3).reshape(tokens_own, chips * pair)
    return grad_hidden, grad_head, (norm_sum - picked) / count


def on_device(hidden, head, targets, log_norm, loss_scale):
    half = head.shape[0] // 2
    tokens_own = hidden.shape[0]
    chips = lax.axis_size(CHIPS)
    shares = lax.axis_size(VOCAB)
    core = lax.axis_index("c")
    span = chips * tokens_own

    chunk = half // RING
    z = lax.axis_index("z")

    sent, head = lax.optimization_barrier((outbox(hidden, targets, log_norm, chips), head))
    got = exchange(sent, CHIPS)

    own = lax.dynamic_slice_in_dim(head, core * half, half, 0)
    away = lax.dynamic_slice_in_dim(head, (1 - core) * half, half, 0)
    wide = lax.optimization_barrier(jnp.concatenate([own, swap(away, "c")], axis=1))
    chunks = [
        lax.dynamic_slice_in_dim(wide, lax.rem(z + d, RING) * chunk, chunk, 0) for d in range(RING)]
    got, wide, chunks = lax.optimization_barrier((got, wide, chunks))
    a = got.reshape(span, -1)
    b = swap(got, "c").reshape(span, -1)

    where = core.reshape(1).astype(jnp.int32)
    box = inbox(where, a, b, PACKED, shares, chips)
    outputs = passes(box, head, wide, chunks, loss_scale, tokens_own)

    def again(state):
        full = inbox(where, a, b, span + 16, shares, chips)
        return (jnp.bool_(False),) + passes(full, head, wide, chunks, loss_scale, tokens_own)

    state = lax.while_loop(lambda state: state[0], again, (box[5][2, 0] >= PACKED,) + outputs)
    return state[1:]


def solution(mesh):
    fine = Mesh(mesh.devices.reshape(2, RING, 2, 2, 4), ("yh", "z", "c", "yl", "x"))
    return jax.shard_map(
        on_device,
        mesh=fine,
        in_specs=(P(DP, None), P(VOCAB, DP), P(DP), P(DP), P()),
        out_specs=(P(DP, None), P(VOCAB, DP), P()),
        check_vma=False,
    )
```

```python
import functools

import jax
import jax.numpy as jnp
from jax import lax
from jax.experimental import pallas as pl
from jax.experimental.pallas import tpu as pltpu
from jax.sharding import Mesh, PartitionSpec as P

F32 = jnp.float32
BF16 = jnp.bfloat16
F16 = jnp.float16
DP = ("yh", "z", "c")
CHIPS = ("yh", "z")
VOCAB = ("yl", "x")
RING = 8
LANES = 128
PACKED = 160
SMEM = pl.BlockSpec(memory_space=pltpu.SMEM)
VMEM = pl.BlockSpec(memory_space=pltpu.VMEM)
ANY = pl.BlockSpec(memory_space=pl.ANY)
HBM = pl.BlockSpec(memory_space=pltpu.HBM)
PARTS = 4
PARAMS = pltpu.CompilerParams(vmem_limit_bytes=12 * 1024 * 1024)
LARGE = pltpu.CompilerParams(vmem_limit_bytes=24 * 1024 * 1024)


def swap(value, axis):
    return lax.ppermute(value, axis, [(0, 1), (1, 0)])


def hop(value, step):
    return lax.ppermute(value, "z", [(i, (i + step) % RING) for i in range(RING)])


def dot(a, b, contract):
    return lax.dot_general(a, b, (contract, ((), ())), preferred_element_type=F32)


def exchange(value, axes):
    return lax.all_to_all(value, axes, split_axis=0, concat_axis=0, tiled=True)


def split(value):
    high = value.astype(BF16)
    rest = value - high.astype(F32)
    mid = rest.astype(BF16)
    return high, mid, (rest - mid.astype(F32)).astype(BF16)


def outbox_kernel(hidden_far, targets_far, norm_far, out, hidden, targets, norm, sems):
    copies = [
        pltpu.make_async_copy(far, near, sems.at[i]) for i, (far, near) in enumerate(
            ((targets_far, targets), (norm_far, norm), (hidden_far, hidden)))]
    for copy in copies:
        copy.start()
    for copy in copies:
        copy.wait()
    tokens = hidden.shape[0]
    chips, _, wide = out.shape
    pair = wide - LANES
    eye = lax.broadcasted_iota(jnp.int32, (tokens, tokens), 0) == lax.broadcasted_iota(
        jnp.int32, (tokens, tokens), 1)
    code = jnp.sum(jnp.where(eye, targets[...] + 1, 0), axis=1, keepdims=True)
    column = jnp.sum(jnp.where(eye, norm[...], 0.0), axis=1, keepdims=True)
    values = [(code >> 8).astype(F32), (code & 255).astype(F32)]
    values += [part.astype(F32) for part in split(column)]
    lane = lax.broadcasted_iota(jnp.int32, (tokens, LANES), 1)
    facts = jnp.zeros((tokens, LANES), F32)
    for i, value in enumerate(values):
        facts = jnp.where(lane == i, value, facts)
    facts = facts.astype(BF16)
    for i in range(chips):
        out[i, :, :pair] = hidden[:, i * pair : (i + 1) * pair]
        out[i, :, pair:] = facts


def outbox(hidden, targets, log_norm, chips):
    tokens, features = hidden.shape
    return pl.pallas_call(
        outbox_kernel,
        out_shape=jax.ShapeDtypeStruct((chips, tokens, features // chips + LANES), BF16),
        in_specs=[HBM] * 3,
        out_specs=VMEM,
        scratch_shapes=[
            pltpu.VMEM((tokens, features), BF16), pltpu.VMEM((1, tokens), jnp.int32),
            pltpu.VMEM((1, tokens), F32), pltpu.SemaphoreType.DMA((3,))],
        compiler_params=PARAMS,
        name="outbox",
    )(hidden, targets[None], log_norm[None])


def inbox_kernel(core, a, b, hid_a, hid_b, facts_a, facts_b, back_far, sums, back, sem, *, shares, chips):
    span, wide = a.shape
    rows = hid_a.shape[0]
    pair = wide - LANES
    half = pair // 2
    tokens = span // chips
    share = tokens // shares
    r = lax.broadcasted_iota(jnp.int32, (span, span), 0)
    c = lax.broadcasted_iota(jnp.int32, (span, span), 1)
    before = (c <= r).astype(F32).astype(BF16)
    slot = lax.broadcasted_iota(jnp.int32, (span, rows), 1).astype(F32)
    counts, norms = [], []
    for x, hid, facts in ((a, hid_a, facts_a), (b, hid_b, facts_b)):
        own = x[:, pair:].astype(F32)
        code = own[:, 0:1] * 256.0 + own[:, 1:2]
        norm = own[:, 2:3] + own[:, 3:4] + own[:, 4:5]
        kept = jnp.where(code > 0.0, 1.0, 0.0)
        rank = dot(before, jnp.broadcast_to(kept, (span, LANES)).astype(BF16), ((1,), (0,)))
        place = jnp.where((rank[:, 0:1] - 1.0 == slot) & (kept > 0.0), 1.0, 0.0).astype(BF16)
        packed = dot(place, x[...], ((0,), (0,)))
        first, second = packed[:, :half], packed[:, half:pair]
        hid[:, :half] = jnp.where(core[0] == 0, first, second).astype(BF16)
        hid[:, half:] = jnp.where(core[0] == 0, second, first).astype(BF16)
        end = packed[:, pair:]
        lane = lax.broadcasted_iota(jnp.int32, (rows, LANES), 1)
        facts[...] = jnp.where(
            lane == 0, end[:, 0:1] * 256.0 + end[:, 1:2] - 1.0,
            jnp.where(lane == 1, end[:, 2:3] + end[:, 3:4] + end[:, 4:5], 0.0))
        counts.append(jnp.sum(kept, axis=0, keepdims=True))
        norms.append(jnp.sum(kept * norm, axis=0, keepdims=True))
        if x is a:
            i, rest = r // (chips * shares), r % (chips * shares)
            source = rest // shares * tokens + rest % shares * share + i
            order = jnp.where(c == source, 1.0, 0.0).astype(BF16)
            back[...] = dot(order, place, ((1,), (0,))).astype(BF16)
            copy = pltpu.make_async_copy(back, back_far, sem)
            copy.start()
    row = lax.broadcasted_iota(jnp.int32, (8, LANES), 0)
    sums[...] = jnp.where(
        row == 0, counts[0] + counts[1],
        jnp.where(row == 1, norms[0] + norms[1], jnp.maximum(counts[0], counts[1])))
    copy.wait()


def inbox(core, a, b, rows, shares, chips):
    span, wide = a.shape
    pair = wide - LANES
    return pl.pallas_call(
        functools.partial(inbox_kernel, shares=shares, chips=chips),
        out_shape=(
            jax.ShapeDtypeStruct((rows, pair), BF16), jax.ShapeDtypeStruct((rows, pair), BF16),
            jax.ShapeDtypeStruct((rows, LANES), F32), jax.ShapeDtypeStruct((rows, LANES), F32),
            jax.ShapeDtypeStruct((span, rows), BF16), jax.ShapeDtypeStruct((8, LANES), F32)),
        in_specs=[SMEM, VMEM, VMEM],
        out_specs=(VMEM,) * 4 + (HBM, VMEM),
        scratch_shapes=[pltpu.VMEM((span, rows), BF16), pltpu.SemaphoreType.DMA],
        compiler_params=PARAMS,
        name="inbox",
    )(core, a, b)


def grad_kernel(first, logits, facts, out):
    rows, chunk = logits.shape
    value = logits[...]
    target, norm = facts[:, 0:1], facts[:, 1:2]
    ids = lax.broadcasted_iota(jnp.int32, (rows, chunk), 1) + first[0]
    onehot = ids.astype(F32) == target
    probs = jnp.exp(value - norm)
    grad = jnp.where(target >= 0.0, probs - jnp.where(onehot, 1.0, 0.0), 0.0)
    picked = jnp.sum(jnp.where(onehot, value, 0.0), axis=1, keepdims=True)
    picked = jnp.sum(picked, axis=0, keepdims=True)
    lane = lax.broadcasted_iota(jnp.int32, (1, chunk), 1)
    last = jnp.zeros((1, chunk), F32)
    for i, part in enumerate(split(picked)):
        last = jnp.where(lane == i, part.astype(F32), last)
    row = lax.broadcasted_iota(jnp.int32, (rows, chunk), 0)
    out[...] = jnp.where(row == rows - 1, last, grad).astype(BF16)


def grad_of(first, logits, facts):
    return pl.pallas_call(
        grad_kernel,
        out_shape=jax.ShapeDtypeStruct(logits.shape, BF16),
        in_specs=[SMEM, VMEM, VMEM],
        out_specs=VMEM,
        compiler_params=PARAMS,
        name="grad",
    )(first, logits, facts)


def chunk_copies(core, z, head, seen, held, sems, slot, distance):
    chunk, width = held.shape[1], head.shape[1]
    at = core[0] * (head.shape[0] // 2) + lax.rem(z[0] + distance, RING) * chunk
    at = pl.multiple_of(at, chunk)
    return [
        pltpu.make_async_copy(
            block.at[pl.ds(at, chunk)], held.at[slot, :, pl.ds(i * width, width)],
            sems.at[slot, i])
        for i, block in enumerate((head, seen))]


def own_terms(core, z, hid, head, seen, wanted):
    distances = list(dict.fromkeys(d for _, d in wanted))
    rows, pair = hid[0].shape
    chunk = head.shape[0] // 2 // RING

    def kernel(core, z, hid_a, hid_b, head, seen, *refs):
        outs, (held, sems) = refs[: len(wanted)], refs[len(wanted) :]
        copies = [
            chunk_copies(core, z, head, seen, held, sems, slot, d)
            for slot, d in enumerate(distances)]
        for pair in copies:
            for copy in pair:
                copy.start()
        for slot, d in enumerate(distances):
            for copy in copies[slot]:
                copy.wait()
            for (s, distance), out in zip(wanted, outs):
                if distance == d:
                    out[...] = dot((hid_a, hid_b)[s][...], held[slot], ((1,), (1,)))

    outs = pl.pallas_call(
        kernel,
        out_shape=(jax.ShapeDtypeStruct((rows, chunk), F32),) * len(wanted),
        in_specs=[SMEM, SMEM, VMEM, VMEM, HBM, HBM],
        out_specs=(VMEM,) * len(wanted),
        scratch_shapes=[
            pltpu.VMEM((len(distances), chunk, pair), BF16),
            pltpu.SemaphoreType.DMA((len(distances), 2))],
        compiler_params=LARGE,
        cost_estimate=pl.CostEstimate(
            flops=2 * rows * chunk * pair * len(wanted), bytes_accessed=len(wanted) << 20,
            transcendentals=0),
        name="own_terms",
    )(core, z, *hid, head, seen)
    return dict(zip(wanted, outs))


def hidden_rows(earlier, pieces, core, z, head, seen, distances):
    count = len(pieces) // 2
    rows, chunk = pieces[0].shape
    pair = 2 * head.shape[1]

    def kernel(core, z, head, seen, *refs):
        pieces, before = refs[: 2 * count], refs[2 * count : 2 * count + len(earlier)]
        out_a, out_b, held, sems = refs[2 * count + len(earlier) :]
        copies = [
            chunk_copies(core, z, head, seen, held, sems, slot, d)
            for slot, d in enumerate(distances)]
        for both in copies:
            for copy in both:
                copy.start()
        total = [ref[...] for ref in before]
        picked = total[1][rows - 1 :, 0:1] if total else jnp.zeros((1, 1), F32)
        row = lax.broadcasted_iota(jnp.int32, (16, LANES), 0)
        lane = lax.broadcasted_iota(jnp.int32, (16, LANES), 1)
        for d in range(count):
            for copy in copies[d]:
                copy.wait()
            for s in range(2):
                piece = pieces[s * count + d]
                term = dot(piece[...], held[d], ((1,), (0,)))
                total = total + [term] if len(total) < 2 else [
                    t + term if i == s else t for i, t in enumerate(total)]
                end = piece[rows - 16 :, :LANES].astype(F32)
                end = jnp.where((row == 15) & (lane < 3), end, 0.0)
                picked += jnp.sum(jnp.sum(end, axis=1, keepdims=True), axis=0, keepdims=True)
        out_a[...] = total[0]
        last = lax.broadcasted_iota(jnp.int32, (rows, pair), 0) == rows - 1
        out_b[...] = jnp.where(last, picked, total[1])

    return pl.pallas_call(
        kernel,
        out_shape=(jax.ShapeDtypeStruct((rows, pair), F32),) * 2,
        in_specs=[SMEM, SMEM, HBM, HBM] + [VMEM] * (2 * count + len(earlier)),
        out_specs=(VMEM, VMEM),
        scratch_shapes=[
            pltpu.VMEM((count, chunk, pair), BF16), pltpu.SemaphoreType.DMA((count, 2))],
        compiler_params=LARGE,
        cost_estimate=pl.CostEstimate(
            flops=4 * rows * chunk * pair * count, bytes_accessed=count << 20, transcendentals=0),
        name="hidden_rows",
    )(core, z, head, seen, *pieces, *earlier)


def terms_kernel(core, mine, own_b, other, back_far, out, picked, back, sem):
    copy = pltpu.make_async_copy(back_far, back, sem)
    copy.start()
    rows, pair = mine.shape
    half = pair // 2
    share = 8 // (pair // LANES)
    parts = [
        split(mine[:, at : at + half] + other[:, seen : seen + half])
        for at, seen in ((0, half), (half, 0))]
    copy.wait()
    own = back[...]
    full = [sum(dot(own, part, ((1,), (0,))) for part in side) for side in parts]
    natural = (jnp.where(core[0] == 0, full[0], full[1]), jnp.where(core[0] == 0, full[1], full[0]))
    blocks = own.shape[0] // share
    tiles = pair // LANES
    for i in range(share):
        for j in range(tiles):
            side = natural[j * LANES // half]
            at = j * LANES % half
            out[pl.ds(i * tiles + j, blocks, stride=share * tiles), :] = side[
                i * blocks : (i + 1) * blocks, at : at + LANES]
    picked[...] = jnp.broadcast_to(
        own_b[rows - 1 :, :LANES] + other[rows - 1 :, :LANES], picked.shape)


def terms_of(core, mine, own_b, other, back):
    span, pair = back.shape[0], mine.shape[1]
    return pl.pallas_call(
        terms_kernel,
        out_shape=(
            jax.ShapeDtypeStruct((span * pair // LANES, LANES), F32),
            jax.ShapeDtypeStruct((8, LANES), F32)),
        in_specs=[SMEM] + [VMEM] * 3 + [HBM],
        out_specs=(VMEM, VMEM),
        scratch_shapes=[pltpu.VMEM(back.shape, BF16), pltpu.SemaphoreType.DMA],
        compiler_params=PARAMS,
        name="terms",
    )(core, mine, own_b, other, back)


def collect_kernel(scale, terms, picked, out):
    chips = terms.shape[0] // 64
    total = jnp.sum(terms[...].reshape(chips, 8, 8, LANES), axis=1).reshape(chips * 8, LANES)
    value = (total * scale[0]).astype(BF16)
    row = lax.broadcasted_iota(jnp.int32, (16, LANES), 0)
    parts = jnp.zeros((16, LANES), F32)
    for i, part in enumerate(split(picked[0:1, :])):
        parts = jnp.where(row == i, part.astype(F32), parts)
    for w in range(out.shape[0]):
        out[w, : chips * 8] = value
        out[w, chips * 8 :] = parts.astype(BF16)


def collect(factor, terms, picked, shares, chips):
    return pl.pallas_call(
        collect_kernel,
        out_shape=jax.ShapeDtypeStruct((shares, chips * 8 + 16, LANES), BF16),
        in_specs=[SMEM, VMEM, VMEM],
        out_specs=VMEM,
        compiler_params=PARAMS,
        name="collect",
    )(factor.reshape(1), terms, picked)


def loss_kernel(ends, sums, out):
    row = lax.broadcasted_iota(jnp.int32, (16, LANES), 0)
    at = ends.shape[1] - 16
    total = jnp.zeros((16, LANES), F32)
    for w in range(ends.shape[0]):
        total += ends[w, at:, :].astype(F32)
    picked = jnp.sum(jnp.where(row < 3, total, 0.0), axis=0, keepdims=True)
    out[...] = (sums[1:2, 0:1] - picked[:, 0:1]) / sums[0:1, 0:1]


def loss_of(ends, sums):
    return pl.pallas_call(
        loss_kernel,
        out_shape=jax.ShapeDtypeStruct((1, 1), F32),
        in_specs=[VMEM, VMEM],
        out_specs=VMEM,
        compiler_params=PARAMS,
        name="loss",
    )(ends, sums).reshape(())


def head_rows(pieces, hid, factor, core, z, rows, width):
    half = rows // 2
    chunk = half // RING

    tokens = hid[0].shape[0]
    part = half // PARTS

    def kernel(z, core, scale, *refs):
        pieces, refs = refs[: 2 * RING], refs[2 * RING :]
        hid_a, hid_b, own, refs = refs[0], refs[1], refs[2], refs[3:]
        gives, (near, held, sems, far_sems) = refs[:PARTS], refs[PARTS:]

        def fetch(d):
            return [
                pltpu.make_async_copy(
                    pieces[s * RING + d], near.at[d % 2, s], far_sems.at[d % 2, s])
                for s in range(2)]

        for copy in fetch(0):
            copy.start()
        for d in range(RING):
            slot = d % 2
            at = pl.multiple_of(lax.rem(z[0] + d, RING) * chunk, chunk)
            if d + 1 < RING:
                for copy in fetch(d + 1):
                    copy.start()
            for copy in fetch(d):
                copy.wait()
            made = dot(near[slot, 0], hid_a[...], ((0,), (0,)))
            made += dot(near[slot, 1], hid_b[...], ((0,), (0,)))
            if d >= 2:
                for i in range(2):
                    pltpu.make_async_copy(
                        held.at[slot, :, pl.ds(i * width, width)],
                        own.at[pl.ds(0, chunk)], sems.at[slot, i]).wait()
            held[slot] = (made * scale[0]).astype(BF16)
            pltpu.make_async_copy(
                held.at[slot, :, pl.ds(0, width)],
                own.at[pl.ds(pl.multiple_of(core[0] * half + at, chunk), chunk)],
                sems.at[slot, 0]).start()
            for i, give in enumerate(gives):
                inside = at - i * part

                @pl.when((inside >= 0) & (inside < part))
                def _(give=give, inside=inside):
                    pltpu.make_async_copy(
                        held.at[slot, :, pl.ds(width, width)],
                        give.at[pl.ds(pl.multiple_of(inside, chunk), chunk)],
                        sems.at[slot, 1]).start()
        for slot in range(2):
            for i in range(2):
                pltpu.make_async_copy(
                    held.at[slot, :, pl.ds(i * width, width)],
                    own.at[pl.ds(0, chunk)], sems.at[slot, i]).wait()

    return pl.pallas_call(
        kernel,
        out_shape=(jax.ShapeDtypeStruct((rows, width), BF16),)
        + (jax.ShapeDtypeStruct((part, width), BF16),) * PARTS,
        in_specs=[SMEM] * 3 + [ANY] * (2 * RING) + [VMEM] * 2,
        out_specs=(ANY,) * (1 + PARTS),
        scratch_shapes=[
            pltpu.VMEM((2, 2, tokens, chunk), BF16),
            pltpu.VMEM((2, chunk, 2 * width), BF16),
            pltpu.SemaphoreType.DMA((2, 2)),
            pltpu.SemaphoreType.DMA((2, 2)),
        ],
        compiler_params=LARGE,
        cost_estimate=pl.CostEstimate(
            flops=4 * hid[0].shape[0] * half * 2 * width, bytes_accessed=9 << 20, transcendentals=0),
        name="head_rows",
    )(z, core, factor.reshape(1), *pieces, *hid)


def passes(box, head, seen, loss_scale, tokens_own):
    hid, facts, back, sums = box[:2], box[2:4], box[4], box[5]
    rows, width = head.shape
    half = rows // 2
    chunk = half // RING
    pair = 2 * width
    chips = lax.axis_size(CHIPS)
    shares = lax.axis_size(VOCAB)
    core = lax.axis_index("c")
    z = lax.axis_index("z")
    share = tokens_own // shares
    factor = loss_scale / sums[0, 0]
    where = core.reshape(1).astype(jnp.int32)
    first = (lax.axis_index(VOCAB) * rows + core * half + z * chunk).reshape(1).astype(jnp.int32)
    here = z.reshape(1).astype(jnp.int32)

    starts = (((0, 4), (1, 4)), ((0, 5), (1, 3)))
    others = ((0, 3), (1, 5), (0, 6), (1, 2), (0, 2), (1, 6), (0, 7), (1, 1), (0, 1), (1, 7), (0, 0), (1, 0))
    terms = {}
    for wanted in starts + (others,):
        terms.update(own_terms(where, here, hid, head, seen, wanted))
    grad = []
    for s in range(2):
        way = 1 if s == 0 else -1
        total = terms[s, 0]
        for direction, length in ((way, RING // 2), (-way, RING // 2 - 1)):
            arrived = None
            for distance in range(length, 0, -1):
                term = terms[s, direction * distance % RING]
                if arrived is not None:
                    term = term + arrived.astype(F32)
                arrived = hop(term.astype(F16), direction)
            total = total + arrived.astype(F32)
        logits = total + swap(total.astype(F16), "yh").astype(F32)
        grad.append(grad_of(first, logits, facts[s]))

    pieces = {}
    for s in range(2):
        way = 1 if s == 0 else -1
        pieces[s, 0] = grad[s]
        for direction in (way, -way):
            for distance in range(1, RING // 2):
                pieces[s, -direction * distance % RING] = hop(
                    pieces[s, -direction * (distance - 1) % RING], direction)

    def batch(earlier, distances):
        return hidden_rows(
            earlier, [pieces[s, d] for s in range(2) for d in distances], where, here, head, seen,
            distances)

    hidden_grad = batch((), (0, 1, 7, 2, 6))
    near, away, hidden_grad = lax.optimization_barrier((pieces[0, 5], pieces[1, 3], hidden_grad))
    pieces[0, 4], pieces[1, 4] = hop(near, 1), hop(away, -1)
    hidden_grad = batch(hidden_grad, (3, 5, 4))

    other = swap(hidden_grad[1], "c")
    terms, picked = terms_of(where, hidden_grad[0], hidden_grad[1], other, back)
    terms, held = lax.optimization_barrier(
        (terms, [pieces[s, d] for s in range(2) for d in range(RING)]))
    grad_head, *give = head_rows(held, hid, factor, where, here, rows, width)
    terms = exchange(terms.reshape(chips * shares, 8, LANES), CHIPS + VOCAB)
    mine = collect(factor, terms.reshape(-1, LANES), picked, shares, chips)
    ends = exchange(mine, VOCAB)
    given = jnp.concatenate([swap(part, "c") for part in give], axis=0)
    grad_head = lax.dynamic_update_slice_in_dim(grad_head, given, (1 - core) * half, 0)
    loss = loss_of(ends, sums)
    tiles = pair // LANES
    ends = ends[:, : chips * 8].reshape(shares, chips, share, tiles * LANES)
    grad_hidden = ends.transpose(0, 2, 1, 3).reshape(tokens_own, chips * pair)
    return grad_hidden, grad_head, loss


def on_device(hidden, head, targets, log_norm, loss_scale):
    tokens_own = hidden.shape[0]
    chips = lax.axis_size(CHIPS)
    shares = lax.axis_size(VOCAB)
    core = lax.axis_index("c")
    span = chips * tokens_own

    got = exchange(outbox(hidden, targets, log_norm, chips), CHIPS)

    seen = swap(head, "c")
    a = got.reshape(span, -1)
    b = swap(got, "c").reshape(span, -1)

    where = core.reshape(1).astype(jnp.int32)
    box = inbox(where, a, b, PACKED, shares, chips)
    outputs = passes(box, head, seen, loss_scale, tokens_own)

    def again(state):
        full = inbox(where, a, b, span + 16, shares, chips)
        return (jnp.bool_(False),) + passes(full, head, seen, loss_scale, tokens_own)

    state = lax.while_loop(lambda state: state[0], again, (box[5][2, 0] >= PACKED,) + outputs)
    return state[1:]


def solution(mesh):
    fine = Mesh(mesh.devices.reshape(2, RING, 2, 2, 4), ("yh", "z", "c", "yl", "x"))
    return jax.shard_map(
        on_device,
        mesh=fine,
        in_specs=(P(DP, None), P(VOCAB, DP), P(DP), P(DP), P()),
        out_specs=(P(DP, None), P(VOCAB, DP), P()),
        check_vma=False,
    )
```

```python
import functools

import jax
import jax.numpy as jnp
from jax import lax
from jax.experimental import pallas as pl
from jax.experimental.pallas import tpu as pltpu
from jax.sharding import Mesh, PartitionSpec as P

F32 = jnp.float32
BF16 = jnp.bfloat16
F16 = jnp.float16
DP = ("yh", "z", "c")
CHIPS = ("yh", "z")
VOCAB = ("yl", "x")
RING = 8
LANES = 128
PACKED = 160
SMEM = pl.BlockSpec(memory_space=pltpu.SMEM)
VMEM = pl.BlockSpec(memory_space=pltpu.VMEM)
ANY = pl.BlockSpec(memory_space=pl.ANY)
HBM = pl.BlockSpec(memory_space=pltpu.HBM)
PARTS = 4
PARAMS = pltpu.CompilerParams(vmem_limit_bytes=12 * 1024 * 1024)
LARGE = pltpu.CompilerParams(vmem_limit_bytes=24 * 1024 * 1024)


def swap(value, axis):
    return lax.ppermute(value, axis, [(0, 1), (1, 0)])


def hop(value, step):
    return lax.ppermute(value, "z", [(i, (i + step) % RING) for i in range(RING)])


def dot(a, b, contract):
    return lax.dot_general(a, b, (contract, ((), ())), preferred_element_type=F32)


def exchange(value, axes):
    return lax.all_to_all(value, axes, split_axis=0, concat_axis=0, tiled=True)


def split(value):
    high = value.astype(BF16)
    rest = value - high.astype(F32)
    mid = rest.astype(BF16)
    return high, mid, (rest - mid.astype(F32)).astype(BF16)


def outbox_kernel(hidden_far, targets_far, norm_far, out, hidden, targets, norm, sems):
    copies = [
        pltpu.make_async_copy(far, near, sems.at[i]) for i, (far, near) in enumerate(
            ((targets_far, targets), (norm_far, norm), (hidden_far, hidden)))]
    for copy in copies:
        copy.start()
    for copy in copies:
        copy.wait()
    tokens = hidden.shape[0]
    chips, _, wide = out.shape
    pair = wide - LANES
    eye = lax.broadcasted_iota(jnp.int32, (tokens, tokens), 0) == lax.broadcasted_iota(
        jnp.int32, (tokens, tokens), 1)
    code = jnp.sum(jnp.where(eye, targets[...] + 1, 0), axis=1, keepdims=True)
    column = jnp.sum(jnp.where(eye, norm[...], 0.0), axis=1, keepdims=True)
    values = [(code >> 8).astype(F32), (code & 255).astype(F32)]
    values += [part.astype(F32) for part in split(column)]
    lane = lax.broadcasted_iota(jnp.int32, (tokens, LANES), 1)
    facts = jnp.zeros((tokens, LANES), F32)
    for i, value in enumerate(values):
        facts = jnp.where(lane == i, value, facts)
    facts = facts.astype(BF16)
    for i in range(chips):
        out[i, :, :pair] = hidden[:, i * pair : (i + 1) * pair]
        out[i, :, pair:] = facts


def outbox(hidden, targets, log_norm, chips):
    tokens, features = hidden.shape
    return pl.pallas_call(
        outbox_kernel,
        out_shape=jax.ShapeDtypeStruct((chips, tokens, features // chips + LANES), BF16),
        in_specs=[HBM] * 3,
        out_specs=VMEM,
        scratch_shapes=[
            pltpu.VMEM((tokens, features), BF16), pltpu.VMEM((1, tokens), jnp.int32),
            pltpu.VMEM((1, tokens), F32), pltpu.SemaphoreType.DMA((3,))],
        compiler_params=PARAMS,
        name="outbox",
    )(hidden, targets[None], log_norm[None])


def inbox_kernel(core, a, b, hid, facts, back_far, sums, back, sem, *, shares, chips):
    span, wide = a.shape
    rows = hid.shape[1]
    pair = wide - LANES
    half = pair // 2
    tokens = span // chips
    share = tokens // shares
    r = lax.broadcasted_iota(jnp.int32, (span, span), 0)
    c = lax.broadcasted_iota(jnp.int32, (span, span), 1)
    before = (c <= r).astype(F32).astype(BF16)
    slot = lax.broadcasted_iota(jnp.int32, (span, rows), 1).astype(F32)
    counts, norms = [], []
    for s, x in enumerate((a, b)):
        own = x[:, pair:].astype(F32)
        code = own[:, 0:1] * 256.0 + own[:, 1:2]
        norm = own[:, 2:3] + own[:, 3:4] + own[:, 4:5]
        kept = jnp.where(code > 0.0, 1.0, 0.0)
        rank = dot(before, jnp.broadcast_to(kept, (span, LANES)).astype(BF16), ((1,), (0,)))
        place = jnp.where((rank[:, 0:1] - 1.0 == slot) & (kept > 0.0), 1.0, 0.0).astype(BF16)
        packed = dot(place, x[...], ((0,), (0,)))
        first, second = packed[:, :half], packed[:, half:pair]
        hid[s, :, :half] = jnp.where(core[0] == 0, first, second).astype(BF16)
        hid[s, :, half:] = jnp.where(core[0] == 0, second, first).astype(BF16)
        end = packed[:, pair:]
        lane = lax.broadcasted_iota(jnp.int32, (rows, LANES), 1)
        facts[s] = jnp.where(
            lane == 0, end[:, 0:1] * 256.0 + end[:, 1:2] - 1.0,
            jnp.where(lane == 1, end[:, 2:3] + end[:, 3:4] + end[:, 4:5], 0.0))
        counts.append(jnp.sum(kept, axis=0, keepdims=True))
        norms.append(jnp.sum(kept * norm, axis=0, keepdims=True))
        if s == 0:
            i, rest = r // (chips * shares), r % (chips * shares)
            source = rest // shares * tokens + rest % shares * share + i
            order = jnp.where(c == source, 1.0, 0.0).astype(BF16)
            back[...] = dot(order, place, ((1,), (0,))).astype(BF16)
            copy = pltpu.make_async_copy(back, back_far, sem)
            copy.start()
    row = lax.broadcasted_iota(jnp.int32, (8, LANES), 0)
    sums[...] = jnp.where(
        row == 0, counts[0] + counts[1],
        jnp.where(row == 1, norms[0] + norms[1], jnp.maximum(counts[0], counts[1])))
    copy.wait()


def inbox(core, a, b, rows, shares, chips):
    span, wide = a.shape
    pair = wide - LANES
    return pl.pallas_call(
        functools.partial(inbox_kernel, shares=shares, chips=chips),
        out_shape=(
            jax.ShapeDtypeStruct((2, rows, pair), BF16),
            jax.ShapeDtypeStruct((2, rows, LANES), F32),
            jax.ShapeDtypeStruct((span, rows), BF16), jax.ShapeDtypeStruct((8, LANES), F32)),
        in_specs=[SMEM, VMEM, VMEM],
        out_specs=(VMEM, VMEM, HBM, VMEM),
        scratch_shapes=[pltpu.VMEM((span, rows), BF16), pltpu.SemaphoreType.DMA],
        compiler_params=PARAMS,
        name="inbox",
    )(core, a, b)


def grad_kernel(first, logits, facts, out):
    rows, chunk = logits.shape
    value = logits[...]
    target, norm = facts[:, 0:1], facts[:, 1:2]
    ids = lax.broadcasted_iota(jnp.int32, (rows, chunk), 1) + first[0]
    onehot = ids.astype(F32) == target
    probs = jnp.exp(value - norm)
    grad = jnp.where(target >= 0.0, probs - jnp.where(onehot, 1.0, 0.0), 0.0)
    picked = jnp.sum(jnp.where(onehot, value, 0.0), axis=1, keepdims=True)
    picked = jnp.sum(picked, axis=0, keepdims=True)
    lane = lax.broadcasted_iota(jnp.int32, (1, chunk), 1)
    last = jnp.zeros((1, chunk), F32)
    for i, part in enumerate(split(picked)):
        last = jnp.where(lane == i, part.astype(F32), last)
    row = lax.broadcasted_iota(jnp.int32, (rows, chunk), 0)
    out[...] = jnp.where(row == rows - 1, last, grad).astype(BF16)


def grad_of(first, logits, facts):
    return pl.pallas_call(
        grad_kernel,
        out_shape=jax.ShapeDtypeStruct(logits.shape, BF16),
        in_specs=[SMEM, VMEM, VMEM],
        out_specs=VMEM,
        compiler_params=PARAMS,
        name="grad",
    )(first, logits, facts)


def chunk_copies(core, z, head, seen, held, sems, slot, distance):
    chunk, width = held.shape[1], head.shape[1]
    at = core[0] * (head.shape[0] // 2) + lax.rem(z[0] + distance, RING) * chunk
    at = pl.multiple_of(at, chunk)
    return [
        pltpu.make_async_copy(
            block.at[pl.ds(at, chunk)], held.at[slot, :, pl.ds(i * width, width)],
            sems.at[slot, i])
        for i, block in enumerate((head, seen))]


def own_terms(core, z, hid, head, seen, distances):
    count = len(distances)
    loads = sorted({d for d in distances} | {-d % RING for d in distances})
    rows, pair = hid.shape[1:]
    chunk = head.shape[0] // 2 // RING

    def kernel(core, z, hid, head, seen, out, held, sems):
        copies = [chunk_copies(core, z, head, seen, held, sems, d, d) for d in loads]
        for both in copies:
            for copy in both:
                copy.start()
        for both in copies:
            for copy in both:
                copy.wait()

        def step(k, carry):
            distance = distances[0] + k
            if count > 1:
                distance = jnp.where(k >= 4, k + 2, k)
            for s, d in ((0, distance), (1, lax.rem(RING - distance, RING))):
                out[k, s] = dot(hid[s], held[d], ((1,), (1,)))
            return carry

        lax.fori_loop(0, count, step, 0)

    return pl.pallas_call(
        kernel,
        out_shape=jax.ShapeDtypeStruct((count, 2, rows, chunk), F32),
        in_specs=[SMEM, SMEM, VMEM, HBM, HBM],
        out_specs=VMEM,
        scratch_shapes=[
            pltpu.VMEM((RING, chunk, pair), BF16), pltpu.SemaphoreType.DMA((RING, 2))],
        compiler_params=LARGE,
        cost_estimate=pl.CostEstimate(
            flops=4 * rows * chunk * pair * count, bytes_accessed=count << 20, transcendentals=0),
        name="own_terms",
    )(core, z, hid, head, seen)


def hidden_rows(earlier, pieces, core, z, head, seen, distances):
    count = len(pieces) // 2
    rows, chunk = pieces[0].shape
    pair = 2 * head.shape[1]

    def kernel(core, z, head, seen, *refs):
        pieces, before = refs[: 2 * count], refs[2 * count : 2 * count + len(earlier)]
        out_a, out_b, held, sems = refs[2 * count + len(earlier) :]
        copies = [
            chunk_copies(core, z, head, seen, held, sems, slot, d)
            for slot, d in enumerate(distances)]
        for both in copies:
            for copy in both:
                copy.start()
        total = [ref[...] for ref in before]
        picked = total[1][rows - 1 :, 0:1] if total else jnp.zeros((1, 1), F32)
        row = lax.broadcasted_iota(jnp.int32, (16, LANES), 0)
        lane = lax.broadcasted_iota(jnp.int32, (16, LANES), 1)
        for d in range(count):
            for copy in copies[d]:
                copy.wait()
            for s in range(2):
                piece = pieces[s * count + d]
                term = dot(piece[...], held[d], ((1,), (0,)))
                total = total + [term] if len(total) < 2 else [
                    t + term if i == s else t for i, t in enumerate(total)]
                end = piece[rows - 16 :, :LANES].astype(F32)
                end = jnp.where((row == 15) & (lane < 3), end, 0.0)
                picked += jnp.sum(jnp.sum(end, axis=1, keepdims=True), axis=0, keepdims=True)
        out_a[...] = total[0]
        last = lax.broadcasted_iota(jnp.int32, (rows, pair), 0) == rows - 1
        out_b[...] = jnp.where(last, picked, total[1])

    return pl.pallas_call(
        kernel,
        out_shape=(jax.ShapeDtypeStruct((rows, pair), F32),) * 2,
        in_specs=[SMEM, SMEM, HBM, HBM] + [VMEM] * (2 * count + len(earlier)),
        out_specs=(VMEM, VMEM),
        scratch_shapes=[
            pltpu.VMEM((count, chunk, pair), BF16), pltpu.SemaphoreType.DMA((count, 2))],
        compiler_params=LARGE,
        cost_estimate=pl.CostEstimate(
            flops=4 * rows * chunk * pair * count, bytes_accessed=count << 20, transcendentals=0),
        name="hidden_rows",
    )(core, z, head, seen, *pieces, *earlier)


def terms_kernel(core, mine, own_b, other, back_far, out, picked, back, sem):
    copy = pltpu.make_async_copy(back_far, back, sem)
    copy.start()
    rows, pair = mine.shape
    half = pair // 2
    share = 8 // (pair // LANES)
    parts = [
        split(mine[:, at : at + half] + other[:, seen : seen + half])
        for at, seen in ((0, half), (half, 0))]
    copy.wait()
    own = back[...]
    full = [sum(dot(own, part, ((1,), (0,))) for part in side) for side in parts]
    natural = (jnp.where(core[0] == 0, full[0], full[1]), jnp.where(core[0] == 0, full[1], full[0]))
    blocks = own.shape[0] // share
    tiles = pair // LANES
    for i in range(share):
        for j in range(tiles):
            side = natural[j * LANES // half]
            at = j * LANES % half
            out[pl.ds(i * tiles + j, blocks, stride=share * tiles), :] = side[
                i * blocks : (i + 1) * blocks, at : at + LANES]
    picked[...] = jnp.broadcast_to(
        own_b[rows - 1 :, :LANES] + other[rows - 1 :, :LANES], picked.shape)


def terms_of(core, mine, own_b, other, back):
    span, pair = back.shape[0], mine.shape[1]
    return pl.pallas_call(
        terms_kernel,
        out_shape=(
            jax.ShapeDtypeStruct((span * pair // LANES, LANES), F32),
            jax.ShapeDtypeStruct((8, LANES), F32)),
        in_specs=[SMEM] + [VMEM] * 3 + [HBM],
        out_specs=(VMEM, VMEM),
        scratch_shapes=[pltpu.VMEM(back.shape, BF16), pltpu.SemaphoreType.DMA],
        compiler_params=PARAMS,
        name="terms",
    )(core, mine, own_b, other, back)


def collect_kernel(scale, terms, picked, out):
    chips = terms.shape[0] // 64
    total = jnp.sum(terms[...].reshape(chips, 8, 8, LANES), axis=1).reshape(chips * 8, LANES)
    value = (total * scale[0]).astype(BF16)
    row = lax.broadcasted_iota(jnp.int32, (16, LANES), 0)
    parts = jnp.zeros((16, LANES), F32)
    for i, part in enumerate(split(picked[0:1, :])):
        parts = jnp.where(row == i, part.astype(F32), parts)
    for w in range(out.shape[0]):
        out[w, : chips * 8] = value
        out[w, chips * 8 :] = parts.astype(BF16)


def collect(factor, terms, picked, shares, chips):
    return pl.pallas_call(
        collect_kernel,
        out_shape=jax.ShapeDtypeStruct((shares, chips * 8 + 16, LANES), BF16),
        in_specs=[SMEM, VMEM, VMEM],
        out_specs=VMEM,
        compiler_params=PARAMS,
        name="collect",
    )(factor.reshape(1), terms, picked)


def loss_kernel(ends, sums, out):
    row = lax.broadcasted_iota(jnp.int32, (16, LANES), 0)
    at = ends.shape[1] - 16
    total = jnp.zeros((16, LANES), F32)
    for w in range(ends.shape[0]):
        total += ends[w, at:, :].astype(F32)
    picked = jnp.sum(jnp.where(row < 3, total, 0.0), axis=0, keepdims=True)
    out[...] = (sums[1:2, 0:1] - picked[:, 0:1]) / sums[0:1, 0:1]


def loss_of(ends, sums):
    return pl.pallas_call(
        loss_kernel,
        out_shape=jax.ShapeDtypeStruct((1, 1), F32),
        in_specs=[VMEM, VMEM],
        out_specs=VMEM,
        compiler_params=PARAMS,
        name="loss",
    )(ends, sums).reshape(())


def head_rows(pieces, hid, factor, core, z, rows, width):
    half = rows // 2
    chunk = half // RING

    tokens = hid.shape[1]
    part = half // PARTS

    def kernel(z, core, scale, *refs):
        pieces, refs = refs[: 2 * RING], refs[2 * RING :]
        hid, own, gives, (near, held, sems, far_sems) = (
            refs[0], refs[1], refs[2 : 2 + PARTS], refs[2 + PARTS :])

        def fetch(d, s):
            return pltpu.make_async_copy(
                pieces[s * RING + d], near.at[d, pl.ds(s * tokens, tokens)], far_sems.at[d])

        def drain(slot):
            for i in range(2):
                pltpu.make_async_copy(
                    held.at[slot, :, pl.ds(i * width, width)],
                    own.at[pl.ds(0, chunk)], sems.at[slot, i]).wait()

        for d in range(RING):
            for s in range(2):
                fetch(d, s).start()

        def step(d, carry):
            slot = lax.rem(d, 2)
            at = pl.multiple_of(lax.rem(z[0] + d, RING) * chunk, chunk)
            pltpu.make_async_copy(near.at[d], near.at[d], far_sems.at[d]).wait()
            made = dot(near[d], hid[...], ((0,), (0,)))

            @pl.when(d >= 2)
            def _():
                drain(slot)

            held[slot] = (made * scale[0]).astype(BF16)
            pltpu.make_async_copy(
                held.at[slot, :, pl.ds(0, width)],
                own.at[pl.ds(pl.multiple_of(core[0] * half + at, chunk), chunk)],
                sems.at[slot, 0]).start()
            for i, give in enumerate(gives):
                inside = at - i * part

                @pl.when((inside >= 0) & (inside < part))
                def _(give=give, inside=inside):
                    pltpu.make_async_copy(
                        held.at[slot, :, pl.ds(width, width)],
                        give.at[pl.ds(pl.multiple_of(inside, chunk), chunk)],
                        sems.at[slot, 1]).start()
            return carry

        lax.fori_loop(0, RING, step, 0)
        drain(0)
        drain(1)

    return pl.pallas_call(
        kernel,
        out_shape=(jax.ShapeDtypeStruct((rows, width), BF16),)
        + (jax.ShapeDtypeStruct((part, width), BF16),) * PARTS,
        in_specs=[SMEM] * 3 + [ANY] * (2 * RING) + [VMEM],
        out_specs=(ANY,) * (1 + PARTS),
        scratch_shapes=[
            pltpu.VMEM((RING, 2 * tokens, chunk), BF16),
            pltpu.VMEM((2, chunk, 2 * width), BF16),
            pltpu.SemaphoreType.DMA((2, 2)),
            pltpu.SemaphoreType.DMA((RING,)),
        ],
        compiler_params=LARGE,
        cost_estimate=pl.CostEstimate(
            flops=4 * tokens * half * 2 * width, bytes_accessed=9 << 20, transcendentals=0),
        name="head_rows",
    )(z, core, factor.reshape(1), *pieces, hid.reshape(2 * tokens, -1))


def passes(box, head, seen, loss_scale, tokens_own):
    hid, facts, back, sums = box
    rows, width = head.shape
    half = rows // 2
    chunk = half // RING
    pair = 2 * width
    chips = lax.axis_size(CHIPS)
    shares = lax.axis_size(VOCAB)
    core = lax.axis_index("c")
    z = lax.axis_index("z")
    share = tokens_own // shares
    factor = loss_scale / sums[0, 0]
    where = core.reshape(1).astype(jnp.int32)
    first = (lax.axis_index(VOCAB) * rows + core * half + z * chunk).reshape(1).astype(jnp.int32)
    here = z.reshape(1).astype(jnp.int32)

    terms = {}
    for distances in ((4,), (5,), (0, 1, 2, 3, 6, 7)):
        made = own_terms(where, here, hid, head, seen, distances)
        for k, d in enumerate(distances):
            terms[0, d], terms[1, -d % RING] = made[k, 0], made[k, 1]
    arrived = {}
    for step in range(RING // 2):
        lanes = [(s, way) for s in range(2) for way in (1, -1) if step < 3 or way == 1 - 2 * s]
        sums_now = []
        for s, way in lanes:
            distance = RING // 2 - step - (0 if way == 1 - 2 * s else 1)
            term = terms[s, way * distance % RING]
            if step:
                term = term + arrived[s, way].astype(F32)
            sums_now.append(term.astype(F16))
        if step:
            sums_now = lax.optimization_barrier(sums_now)
        for (s, way), value in zip(lanes, sums_now):
            arrived[s, way] = hop(value, way)
    grad = []
    for s in range(2):
        total = terms[s, 0] + arrived[s, 1].astype(F32) + arrived[s, -1].astype(F32)
        logits = total + swap(total.astype(F16), "yh").astype(F32)
        grad.append(grad_of(first, logits, facts[s]))

    pieces = {}
    for s in range(2):
        way = 1 if s == 0 else -1
        pieces[s, 0] = grad[s]
        for direction in (way, -way):
            for distance in range(1, RING // 2):
                pieces[s, -direction * distance % RING] = hop(
                    pieces[s, -direction * (distance - 1) % RING], direction)

    def batch(earlier, distances):
        return hidden_rows(
            earlier, [pieces[s, d] for s in range(2) for d in distances], where, here, head, seen,
            distances)

    hidden_grad = batch((), (0, 1, 7, 2, 6))
    near, away, hidden_grad = lax.optimization_barrier((pieces[0, 5], pieces[1, 3], hidden_grad))
    pieces[0, 4], pieces[1, 4] = hop(near, 1), hop(away, -1)
    hidden_grad = batch(hidden_grad, (3, 5, 4))

    other = swap(hidden_grad[1], "c")
    terms, picked = terms_of(where, hidden_grad[0], hidden_grad[1], other, back)
    terms, held = lax.optimization_barrier(
        (terms, [pieces[s, d] for s in range(2) for d in range(RING)]))
    grad_head, *give = head_rows(held, hid, factor, where, here, rows, width)
    terms = exchange(terms.reshape(chips * shares, 8, LANES), CHIPS + VOCAB)
    mine = collect(factor, terms.reshape(-1, LANES), picked, shares, chips)
    ends = exchange(mine, VOCAB)
    given = jnp.concatenate([swap(part, "c") for part in give], axis=0)
    grad_head = lax.dynamic_update_slice_in_dim(grad_head, given, (1 - core) * half, 0)
    loss = loss_of(ends, sums)
    tiles = pair // LANES
    ends = ends[:, : chips * 8].reshape(shares, chips, share, tiles * LANES)
    grad_hidden = ends.transpose(0, 2, 1, 3).reshape(tokens_own, chips * pair)
    return grad_hidden, grad_head, loss


def on_device(hidden, head, targets, log_norm, loss_scale):
    tokens_own = hidden.shape[0]
    chips = lax.axis_size(CHIPS)
    shares = lax.axis_size(VOCAB)
    core = lax.axis_index("c")
    span = chips * tokens_own

    got = exchange(outbox(hidden, targets, log_norm, chips), CHIPS)

    seen = swap(head, "c")
    a = got.reshape(span, -1)
    b = swap(got, "c").reshape(span, -1)

    where = core.reshape(1).astype(jnp.int32)
    box = inbox(where, a, b, PACKED, shares, chips)
    outputs = passes(box, head, seen, loss_scale, tokens_own)

    def again(state):
        full = inbox(where, a, b, span + 16, shares, chips)
        return (jnp.bool_(False),) + passes(full, head, seen, loss_scale, tokens_own)

    state = lax.while_loop(lambda state: state[0], again, (box[3][2, 0] >= PACKED,) + outputs)
    return state[1:]


def solution(mesh):
    fine = Mesh(mesh.devices.reshape(2, RING, 2, 2, 4), ("yh", "z", "c", "yl", "x"))
    return jax.shard_map(
        on_device,
        mesh=fine,
        in_specs=(P(DP, None), P(VOCAB, DP), P(DP), P(DP), P()),
        out_specs=(P(DP, None), P(VOCAB, DP), P()),
        check_vma=False,
    )
```
